32 devices in a mesh: parts: 2 (over x), img: 16 (over z, y, core).
Axes of the slice: x: 2, y: 2, z: 4, core: 2. Of those that a mesh axis runs over, the one named last changes fastest.
Arguments:
- images: bfloat16 [2048, 16384], P(('parts', 'img')), parts along dimension 0, may hold values from -28 to 28
- groups: int32 [2048], P(('parts', 'img')), parts along dimension 0, may hold values from 0 to 7
- shifts: int32 [18, 2], P('parts'), parts along dimension 0, may hold values from -3 to 3
- volume: bfloat16 [32768, 256], P(('parts', 'img')), parts along dimension 0, may hold values from -6 to 6
- owner: int32 [8192, 1], P('parts'), parts along dimension 0, may hold values from 0 to 15; in each aligned block of 4096 rows (0 to 4095, 4096 to 8191, ...) at most 384 rows name the same one
- local: int32 [8192], P('parts'), parts along dimension 0, may hold values from 0 to 1023
- table_id: int32 [8192], P('parts'), parts along dimension 0, may hold values from 0 to 7
- interp: bfloat16 [8, 128, 128], replicated, may hold values from -0.5 to 0.5
- ctf: float32 [16, 8192], P('parts'), parts along dimension 0, may hold values from 0.2 to 1
Outputs:
- new_map: float32 [32768, 256], P(('parts', 'img')), parts along dimension 0
- evidence: float32 [2048], P(('parts', 'img')), parts along dimension 0
The draws below stay inside these ranges and needn't reach their ends.
There are 2 independent parts, one for each index of `parts`. The reference program is written for one: setup_inputs(seed, part) draws one part's arguments, and reference() takes and returns one part's arrays. A program takes and returns all parts, laid end to end along the dimension named above; an argument that names none is the same for every part. Nothing has to cross between parts.
Inputs may be any that keep to these rules, and one draw needn't show every extreme that they name: `owner`: no slab is named by more than 384 slice blocks, a bound that some block reaches.
All inputs are finite; a program needn't handle non-finite values.
Results may differ from the reference program's by a relative error of at most 0.012.
The reference program's roundings to bfloat16 on the way (of `slices`, `rotated`, `weighted` and `weights`) count: a program that leaves them out, or rounds other values in their place, can miss the bound.
Values may be sent and summed in bfloat16 or wider, within the bound.
No kernel may reach another device: no remote copies, remote signals or barrier semaphores. Data moves between devices by JAX's collectives and lax.ppermute only.
A program may use at most 128 MiB of HBM per device.

```python
import math
import jax
import jax.numpy as jnp
import numpy as np
from jax import lax

BW = 128
KB = 64
R = 64
S = 9
G = 8
NT = 8
IMG_DEV = 64
VB_DEV = 1024
IMAGES = 1024
NV = 16384
RB = 4096
MOST = 384
N_IMG = 16


def draw_images(key, part):
    first_key = jax.random.fold_in(jax.random.fold_in(key, 11), 0)
    return jnp.clip(jax.random.normal(first_key, (IMAGES, KB * 2 * BW), jnp.float32), -6.0, 6.0).astype(jnp.bfloat16)


def set_ends(array, own_key, low, high):
    longest = array.shape.index(max(array.shape))
    spots = []
    for shift in (0, 1):
        where = [jax.random.randint(jax.random.fold_in(own_key, axis), (), 0, length) for axis, length in enumerate(array.shape)]
        where[longest] = (where[longest] + shift) % array.shape[longest]
        spots.append(tuple(where))
    return array.at[spots[0]].set(low).at[spots[1]].set(high)


def block_scale(rng, extent, cuts, low, high):
    level, own = 1.0, jax.random.fold_in(rng, 6)
    for dim, parts in cuts:
        draws = jnp.exp(jax.random.uniform(jax.random.fold_in(own, dim), (parts,), jnp.float32, low / len(cuts), high / len(cuts)))
        level = level * jnp.repeat(draws, extent[dim] // parts).reshape([-1 if axis == dim else 1 for axis in range(len(extent))])
    return level


def assign_block(stream_key, own, number, rows, number_of, top, bound, skew):
    order = jax.random.permutation(stream_key, number_of)
    heavy_load, ordinary = shares(number_of, rows * top, bound, skew, True), shares(number_of, rows * top, bound, skew, False)
    places = jnp.arange(number_of)

    def named(lengths, turn):
        used = int((lengths > 0).sum())
        fixed = max(1, used // 4)
        moved = fixed + (places - fixed + turn * (used - fixed)) % max(1, number_of - fixed)
        return jnp.zeros((number_of,), jnp.int32).at[order[jnp.where(places < fixed, places, moved)]].set(jnp.asarray(lengths, jnp.int32))

    lengths = jnp.where(number % 4 == 0, named(heavy_load, number // 4), named(ordinary, number - number // 4 - 1))
    mixed = jax.random.permutation(jax.random.fold_in(own, 3), number_of)
    source_of, taker = mixed[0:number_of // 2 * 2:2], mixed[1:number_of // 2 * 2:2]
    margin = jnp.minimum(lengths[source_of] - 1, bound - lengths[taker]) // 2
    margin = jnp.where((source_of == order[0]) | (taker == order[0]) | (lengths[taker] == 0), 0, jnp.maximum(margin, 0))
    moved = jax.random.randint(jax.random.fold_in(own, 4), (number_of // 2,), 0, 1 << 20) % (margin + 1)
    lengths = lengths.at[source_of].add(-moved).at[taker].add(moved)
    labels = jnp.searchsorted(jnp.cumsum(lengths), jnp.arange(rows * top), side="right").astype(jnp.int32)
    listing = labels.reshape(top, rows).T
    listing = listing[jax.random.permutation(jax.random.fold_in(own, 1), rows)]
    turn = jax.random.randint(jax.random.fold_in(own, 2), (rows, 1), 0, top)
    return jnp.take_along_axis(listing, (jnp.arange(top)[None, :] + turn) % top, axis=1)


def shares(count, total, reach, lean, full):
    loads = [(1 << 20) // math.isqrt(standing ** lean) + 1 for standing in range(1, count + 1)]
    largest = reach if full else min(reach, max(-(-total // count), total * loads[0] // sum(loads)))
    least = 1 if total - largest >= count - 1 else 0
    counts, surplus = [largest] + [least] * (count - 1), total - largest - least * (count - 1)
    while surplus > 0:
        movable = [i for i in range(1, count) if counts[i] < largest] or [i for i in range(1, count) if counts[i] < reach]
        whole, left = sum([loads[i] for i in movable]), surplus
        for i in movable:
            extra = min(reach - counts[i], max(1, left * loads[i] // whole), surplus)
            counts[i] = counts[i] + extra
            surplus = surplus - extra
    return np.array(counts)


def gaussian(own_key, shape, deviation, most, cuts=(), dtype=jnp.bfloat16):
    gain = block_scale(own_key, shape, cuts, -0.22, 0.18) if cuts else 1.0
    drawn = jax.random.normal(own_key, shape, jnp.float32) * deviation * gain
    return jnp.minimum(jnp.maximum(drawn, -most), most).astype(dtype)


def setup_inputs(seed: int = 0, part: int = 0) -> dict:
    key_list = jax.random.split(jax.random.key(seed), 10)
    own_keys = jax.random.split(jax.random.fold_in(key_list[9], part), 10)
    images = draw_images(jax.random.fold_in(jax.random.fold_in(key_list[9], part), 71), part)
    groups = set_ends(jax.random.randint(own_keys[1], (IMAGES,), 0, G), jax.random.fold_in(own_keys[1], 1), 0, G - 1).astype(jnp.int32)
    shifts = set_ends(jax.random.randint(own_keys[2], (S, 2), -3, 4), jax.random.fold_in(own_keys[2], 1), -3, 3).astype(jnp.int32)
    volume = gaussian(own_keys[3], (NV, 2 * BW), 1.0, 6.0, ((0, 16),))
    owner_keys = jax.random.split(jax.random.fold_in(own_keys[4], 1), RB // RB)
    owner_turns = jax.random.permutation(jax.random.fold_in(own_keys[4], 3), RB // RB)
    owner = jax.vmap(lambda own, number: assign_block(jax.random.fold_in(own_keys[4], 2), own, number, RB, N_IMG, 1, MOST, 0))(owner_keys, owner_turns).reshape((RB, 1))
    local = set_ends(jax.random.randint(own_keys[5], (RB,), 0, VB_DEV), jax.random.fold_in(own_keys[5], 1), 0, VB_DEV - 1).astype(jnp.int32)
    table_id = set_ends(jax.random.randint(own_keys[6], (RB,), 0, NT), jax.random.fold_in(own_keys[6], 1), 0, NT - 1).astype(jnp.int32)
    interp = gaussian(key_list[7], (NT, BW, BW), BW ** -0.5, 0.5)
    ctf = jnp.clip(jax.random.uniform(own_keys[8], (G, KB * BW), jnp.float32, 0.2, 1.0), 0.2, 1.0)
    return {"images": images, "groups": groups, "shifts": shifts, "volume": volume, "owner": owner, "local": local, "table_id": table_id, "interp": interp, "ctf": ctf}


exact_mode = lax.Precision.HIGHEST

def phases(shifts):
    freq_x = (jnp.arange(BW) - BW // 2).astype(jnp.float32)
    freq_y = jnp.arange(KB).astype(jnp.float32)
    shift_x = shifts[:, 0].astype(jnp.float32)
    shift_y = shifts[:, 1].astype(jnp.float32)
    angles = 2.0 * math.pi / BW * (shift_x[:, None, None] * freq_x[None, None, :] + shift_y[:, None, None] * freq_y[None, :, None])
    return (jnp.cos(angles), jnp.sin(angles))

def pick_table(blocks_in, table_ids, interp, adjoint):
    tables = interp.astype(jnp.float32)
    if adjoint:
        expanded = jnp.einsum('ncj,tjv->ntcv', blocks_in, tables, precision=exact_mode)
    else:
        expanded = jnp.einsum('ncv,tjv->ntcj', blocks_in, tables, precision=exact_mode)
    one_hot = (table_ids[:, None] == jnp.arange(interp.shape[0])[None, :]).astype(jnp.float32)
    return lax.optimization_barrier(jnp.sum(expanded * one_hot[:, :, None, None], axis=1))

def score_images(image_rows, group_ids, slices, shifts, ctf):
    refs = slices.shape[0]
    count = image_rows.shape[0]
    cosine, sine_values = phases(shifts)
    slice_values = slices.astype(jnp.float32)
    powers = (slice_values[:, :, 0] ** 2 + slice_values[:, :, 1] ** 2).reshape(refs, KB * BW)
    norm_terms = jnp.dot(ctf * ctf, powers.T, precision=exact_mode)
    one_hot = (group_ids[:, None] == jnp.arange(ctf.shape[0])[None, :]).astype(jnp.float32)
    image_ctf = jnp.dot(one_hot, ctf, precision=exact_mode).reshape(count, KB, 1, BW)
    weighted = (image_rows.astype(jnp.float32).reshape(count, KB, 2, BW) * image_ctf).astype(jnp.bfloat16).reshape(count, KB * 2 * BW)
    image_norms = jnp.dot(one_hot, norm_terms, precision=exact_mode)
    scale_factor = 1.0 / math.sqrt(KB * BW)
    score_list = []
    for number in range(cosine.shape[0]):
        real_part = slice_values[:, :, 0] * cosine[number] - slice_values[:, :, 1] * sine_values[number]
        imag_part = slice_values[:, :, 0] * sine_values[number] + slice_values[:, :, 1] * cosine[number]
        rotated = jnp.stack([real_part, imag_part], axis=2).astype(jnp.bfloat16).reshape(refs, KB * 2 * BW)
        intersection = lax.dot_general(weighted, rotated, (((1,), (1,)), ((), ())), preferred_element_type=jnp.float32)
        score_list.append((intersection - 0.5 * image_norms) * scale_factor)
    scores = jnp.stack(score_list, axis=1)
    maximum = lax.optimization_barrier(jnp.max(scores, axis=(1, 2)))
    exponent = jnp.exp(scores - maximum[:, None, None])
    summed = lax.optimization_barrier(jnp.sum(exponent, axis=(1, 2)))
    evidence = maximum + jnp.log(summed)
    weights = (exponent / summed[:, None, None]).astype(jnp.bfloat16)
    accumulated = jnp.zeros((refs, KB, 2, BW), jnp.float32)
    for number in range(cosine.shape[0]):
        partial_sum = lax.dot_general(weights[:, number, :], weighted, (((0,), (0,)), ((), ())), preferred_element_type=jnp.float32).reshape(refs, KB, 2, BW)
        back_real = partial_sum[:, :, 0] * cosine[number] + partial_sum[:, :, 1] * sine_values[number]
        back_imag = partial_sum[:, :, 1] * cosine[number] - partial_sum[:, :, 0] * sine_values[number]
        accumulated = accumulated + jnp.stack([back_real, back_imag], axis=2)
    return (accumulated, evidence)

def reference(images, groups, shifts, volume, owner, local, table_id, interp, ctf):
    volume_index = (owner[:, 0] * VB_DEV + local).astype(jnp.int32)
    volume_rows = volume[volume_index].astype(jnp.float32).reshape(RB, 2, BW)
    slices = pick_table(volume_rows, table_id, interp, False).astype(jnp.bfloat16).reshape(R, KB, 2, BW)

    def image_block(carried, inputs):
        image_rows, group_ids = inputs
        accumulated, evidence = score_images(image_rows, group_ids, slices, shifts, ctf)
        return (carried + accumulated, evidence)
    start = jnp.zeros((R, KB, 2, BW), jnp.float32)
    sums, evidence = lax.scan(image_block, start, (images.reshape(N_IMG, IMG_DEV, KB * 2 * BW), groups.reshape(N_IMG, IMG_DEV)))
    contrib = pick_table(sums.reshape(RB, 2, BW), table_id, interp, True).reshape(RB, 2 * BW)
    new_map = volume.astype(jnp.float32).at[volume_index].add(contrib)
    return (new_map, evidence.reshape(IMAGES))
```

```python
import functools
import math

import jax
import jax.numpy as jnp
from jax import lax
from jax.experimental import pallas as pl
from jax.experimental.pallas import tpu as pltpu
from jax.sharding import PartitionSpec as P

BW = 128
KB = 64
R = 64
HALF = BW // 2
BLOCKS = R * KB
GROUP = 8

F32 = jnp.float32
BF16 = jnp.bfloat16
NT = (((1,), (1,)), ((), ()))
NN = (((1,), (0,)), ((), ()))


def dot(a, b, dims=NN):
    return lax.dot_general(a, b, dims, preferred_element_type=F32)


def iota(shape, axis):
    return lax.broadcasted_iota(jnp.int32, shape, axis)


def swap_halves(x):
    return pltpu.roll(x, HALF, 1)


def split_halves(real, imag):
    first = iota(real.shape, 1) < HALF
    return (
        jnp.where(first, real, swap_halves(imag)),
        jnp.where(first, swap_halves(real), imag),
    )


def slice_kernel(
    devices, ny, nz, cap, meta, owner, local, table, volume, interp, target, slots, keep, send
):
    me = meta[0]
    z, y, core = meta[1], meta[2], meta[3]
    own = owner[...]
    rows = own.shape[0]
    upper = jnp.where(iota((BW, BW), 0) <= iota((BW, BW), 1), 1.0, 0.0).astype(BF16)
    ones = jnp.ones((BW, BW), BF16)
    lower = jnp.where(iota((rows, rows), 1) < iota((rows, rows), 0), 1.0, 0.0).astype(BF16)

    def rank(d, pos):
        member = jnp.where(own == d, 1.0, 0.0)
        bits = member.astype(BF16)
        inclusive = dot(bits, upper)
        before = dot(lower, dot(bits, ones).astype(BF16))
        return pos + member * (inclusive - 1.0 + before)

    pos = jnp.zeros(own.shape, F32)
    if devices <= 16:
        for d in range(devices):
            pos = rank(d, pos)
    else:
        pos = lax.fori_loop(0, devices, rank, pos)
    pos = pos.astype(jnp.int32)
    shift_y = 1
    shift_z = 1 + (ny.bit_length() - 1)
    rel_core = (own & 1) ^ core
    rel_y = (lax.shift_right_logical(own, shift_y) - y) & (ny - 1)
    rel_z = (lax.shift_right_logical(own, shift_z) - z) & (nz - 1)
    target[...] = ((rel_z * ny + rel_y) * 2 + rel_core) * cap + pos

    mine = jnp.where(own == me, pos, -1)
    slot = iota((cap, BW), 0)
    kind = iota((8, BW), 0)
    loc, tab = local[...], table[...]
    high = lax.shift_right_logical(loc, 8).astype(F32)
    low = (loc & 255).astype(F32)
    tab = tab.astype(F32)
    found = jnp.zeros((cap, 8), F32)
    for g in range(rows):
        row = slice(g, g + 1)
        hot = jnp.where(slot == mine[row], 1.0, 0.0).astype(BF16)
        values = jnp.where(
            kind == 0,
            high[row],
            jnp.where(kind == 1, low[row], jnp.where(kind == 2, tab[row], 1.0)),
        ).astype(BF16)
        found = found + dot(hot, values, NT)
    valid = found[:, 3:4] > 0.5
    place = jnp.where(valid, found[:, 0:1] * 256.0 + found[:, 1:2], -1.0)
    which = found[:, 2:3]
    column = iota((cap, 8), 1)
    slots[...] = jnp.where(column == 0, place, jnp.where(column == 1, which, 0.0))

    depth = volume.shape[0]
    pick = jnp.where(iota((cap, depth), 1) == place.astype(jnp.int32), 1.0, 0.0).astype(BF16)
    voxels = dot(pick, volume[...])
    voxels = jnp.concatenate([voxels[:, :BW], voxels[:, BW:]], axis=0)
    which = jnp.concatenate([which, which], axis=0)
    out = jnp.zeros((2 * cap, BW), F32)
    for t in range(interp.shape[0]):
        out = out + dot(jnp.where(which == float(t), voxels, 0.0).astype(BF16), interp[t], NT)
    left, right = split_halves(out[:cap], out[cap:])
    keep[...] = jnp.where(core == 0, left, right).astype(BF16)
    send[...] = jnp.where(core == 0, right, left).astype(BF16)


def weigh_kernel(meta, images, group, ctf, keep, send, squares):
    core = meta[3]
    count = images.shape[0]
    groups = ctf.shape[0]
    number = jnp.broadcast_to(group[...], (count, BW))

    def body(b, carry):
        lanes = pl.ds(pl.multiple_of(b * BW, BW), BW)
        scale = ctf[:, lanes]
        factor = jnp.zeros((count, BW), F32)
        for g in range(groups):
            factor = jnp.where(number == g, scale[g : g + 1], factor)
        real = images[:, pl.ds(pl.multiple_of(b * 2 * BW, BW), BW)].astype(F32) * factor
        imag = images[:, pl.ds(pl.multiple_of(b * 2 * BW + BW, BW), BW)].astype(F32) * factor
        left, right = split_halves(real, imag)
        keep[:, lanes] = jnp.where(core == 0, left, right).astype(BF16)
        send[:, lanes] = jnp.where(core == 0, right, left).astype(BF16)
        square = scale * scale
        left, right = split_halves(square, square)
        square = jnp.where(core == 0, left, right)
        high = square.astype(BF16)
        rest = square - high.astype(F32)
        squares[:, lanes] = jnp.concatenate([high.astype(F32), rest], axis=0).astype(BF16)
        return carry

    lax.fori_loop(0, KB, body, 0, unroll=2)


def score_kernel(
    order, rows, target, group, cosine, sine, keep, other, squares, *rest
):
    pieces = rest[: len(order)]
    scores, gathered, block, left, power, norms = rest[len(order) :]
    shifts = cosine.shape[1]
    for number, piece in zip(order, pieces):
        gathered[pl.ds(number * rows, rows), :] = piece[...].astype(F32)
    scores[...] = jnp.zeros(scores.shape, F32)
    norms[...] = jnp.zeros(norms.shape, F32)

    def body(group_index, carry):
        for part in range(GROUP):
            b = group_index * GROUP + part
            lanes = slice(part * BW, (part + 1) * BW)
            for r in range(R):
                block[part, r : r + 1, :] = gathered[pl.ds(target[r * KB + b], 1), :]
            value = block[part]
            swapped = swap_halves(value)
            for s in range(shifts):
                turned = value * cosine[b, s : s + 1, :] + swapped * sine[b, s : s + 1, :]
                left[s * R : (s + 1) * R, lanes] = turned.astype(BF16)
            square = value * value
            high = square.astype(BF16)
            power[0:R, lanes] = high
            power[R : 2 * R, lanes] = (square - high.astype(F32)).astype(BF16)
        lanes = pl.ds(pl.multiple_of(group_index * GROUP * BW, BW), GROUP * BW)
        right = jnp.concatenate([keep[:, lanes], other[:, lanes]], axis=0)
        scores[...] += dot(left[...], right, NT)
        norms[...] += dot(power[...], squares[:, lanes], NT)
        return carry

    lax.fori_loop(0, KB // GROUP, body, 0)
    half = squares.shape[0] // 2
    total = norms[...]
    total = total[:R, :half] + total[:R, half:] + total[R:, :half] + total[R:, half:]
    norm = jnp.zeros((R, scores.shape[1]), F32)
    for g in range(half):
        norm = jnp.where(group[...] == g, total[:, g : g + 1], norm)
    for s in range(shifts):
        scores[s * R : (s + 1) * R, :] -= 0.5 * norm


def back_kernel(ny, nz, rows, first, target, mine, theirs, cosine, sine, keep, other, *rest):
    evidence = rest[0]
    by_y = rest[1 : 1 + ny]
    by_z = rest[1 + ny : 1 + ny + nz]
    placed, block = rest[1 + ny + nz :]
    shifts = cosine.shape[1]
    scale = 1.0 / math.sqrt(KB * BW)
    placed[...] = jnp.zeros(placed.shape, F32)
    scores = (mine[...] + swap_halves(theirs[...])) * scale
    top = jnp.max(scores, axis=0, keepdims=True)
    exponent = jnp.exp(scores - top)
    total = jnp.sum(exponent, axis=0, keepdims=True)
    evidence[...] = top + jnp.log(total)
    weights = (exponent / total).astype(BF16)

    def body(pair, carry):
        lanes = pl.ds(pl.multiple_of(pair * 2 * BW, BW), 2 * BW)
        right = jnp.concatenate([keep[:, lanes], other[:, lanes]], axis=0)
        sums = dot(weights, right)
        for part in range(2):
            b = pair * 2 + part
            straight = jnp.zeros((R, BW), F32)
            crossed = jnp.zeros((R, BW), F32)
            for s in range(shifts):
                term = sums[s * R : (s + 1) * R, part * BW : (part + 1) * BW]
                straight = straight + term * cosine[b, s : s + 1, :]
                crossed = crossed + term * sine[b, s : s + 1, :]
            block[part] = straight + swap_halves(crossed)
            for r in range(R):
                placed[pl.ds(target[r * KB + b], 1), :] = block[part, r : r + 1, :]
        return carry

    lax.fori_loop(0, KB // 2, body, 0)
    for kz in range(nz):
        for ky in range(ny):
            start = (kz * ny + ky) * rows
            by_y[ky][kz * first : (kz + 1) * first, :] = placed[start : start + first, :].astype(BF16)
            rest_rows = rows - first
            by_z[kz][ky * rest_rows : (ky + 1) * rest_rows, :] = placed[
                start + first : start + rows, :
            ].astype(BF16)


def adjoint_kernel(meta, place, slots, volume, interp, keep, other, new_map):
    core = meta[3]
    cap = keep.shape[0]
    mine, theirs = keep[...], other[...]
    left = jnp.where(core == 0, mine, theirs)
    right = jnp.where(core == 0, theirs, mine)
    real, imag = split_halves(left, right)
    value = jnp.concatenate([real, imag], axis=0)
    which = slots[:, 1:2]
    which = jnp.concatenate([which, which], axis=0)
    high = value.astype(BF16).astype(F32)
    rest = value - high
    out = jnp.zeros((2 * cap, BW), F32)
    for t in range(interp.shape[0]):
        chosen = which == float(t)
        out = out + dot(jnp.where(chosen, high, 0.0).astype(BF16), interp[t])
        out = out + dot(jnp.where(chosen, rest, 0.0).astype(BF16), interp[t])
    out = jnp.concatenate([out[:cap], out[cap:]], axis=1)
    depth = volume.shape[0]
    spread = jnp.where(
        iota((depth, cap), 0) == place[0:1, :].astype(jnp.int32), 1.0, 0.0
    ).astype(BF16)
    high = out.astype(BF16)
    rest = out - high.astype(F32)
    middle = rest.astype(BF16)
    low = (rest - middle.astype(F32)).astype(BF16)
    new_map[...] = volume[...].astype(F32) + (
        dot(spread, high) + (dot(spread, middle) + dot(spread, low))
    )


SMEM = pl.BlockSpec(memory_space=pltpu.SMEM)
VMEM = pl.BlockSpec(memory_space=pltpu.VMEM)


def call(kernel, in_specs, out_shapes, scratch, flops, touched, name):
    return pl.pallas_call(
        kernel,
        in_specs=in_specs,
        out_specs=[VMEM] * len(out_shapes),
        out_shape=out_shapes,
        scratch_shapes=scratch,
        compiler_params=pltpu.CompilerParams(vmem_limit_bytes=40 * 1024 * 1024),
        cost_estimate=pl.CostEstimate(flops=flops, bytes_accessed=touched, transcendentals=0),
        name=name,
    )


def per_device(images, groups, shifts, volume, owner, local, table_id, interp, ctf):
    devices = lax.axis_size("img")
    chips = devices // 2
    ny = 1 << ((chips.bit_length() - 1) // 2)
    nz = chips // ny
    me = lax.axis_index("img")
    core = me % 2
    y = (me // 2) % ny
    z = me // (2 * ny)
    meta = jnp.stack([me, z, y, core]).astype(jnp.int32)
    cap = max(2, 3 * BLOCKS // (2 * devices))
    rows = 2 * cap
    count = images.shape[0]
    shift_count = shifts.shape[0]
    struct = jax.ShapeDtypeStruct

    def device(dz, dy, dc):
        return (dz * ny + dy) * 2 + dc

    everyone = [(dz, dy, dc) for dz in range(nz) for dy in range(ny) for dc in range(2)]
    core_pairs = [(device(*d), device(d[0], d[1], 1 - d[2])) for d in everyone]

    def along_z(k):
        return [(device(a, b, c), device((a + k) % nz, b, c)) for a, b, c in everyone]

    def along_y(k):
        return [(device(a, b, c), device(a, (b + k) % ny, c)) for a, b, c in everyone]

    def to(array, pairs):
        return lax.ppermute(array, "img", pairs)

    wide = (BLOCKS // BW, BW)
    target, slots, slice_keep, slice_send = call(
        functools.partial(slice_kernel, devices, ny, nz, cap),
        [SMEM] + [VMEM] * 5,
        [
            struct(wide, jnp.int32),
            struct((cap, 8), F32),
            struct((cap, BW), BF16),
            struct((cap, BW), BF16),
        ],
        [],
        10**9,
        10**6,
        "own_slices",
    )(meta, owner.reshape(wide), local.reshape(wide), table_id.reshape(wide), volume, interp)
    target = target.reshape(BLOCKS)
    own_piece = jnp.concatenate([slice_keep, to(slice_send, core_pairs)], axis=0)

    pieces = {(0, 0): own_piece}
    near = sorted(range(1, nz), key=lambda k: min(k, nz - k))
    for ky in range(1, ny):
        pieces[0, ky] = to(own_piece, along_y(-ky))
    for kz in near:
        pieces[kz, 0] = to(own_piece, along_z(-kz))
    for kz in near:
        for ky in range(1, ny):
            pieces[kz, ky] = to(pieces[kz, 0], along_y(-ky))

    weight_keep, weight_send, squares = call(
        weigh_kernel,
        [SMEM] + [VMEM] * 3,
        [
            struct((count, KB * BW), BF16),
            struct((count, KB * BW), BF16),
            struct((2 * ctf.shape[0], KB * BW), BF16),
        ],
        [],
        10**9,
        4 * 10**6,
        "weigh",
    )(meta, images, groups.reshape(count, 1), ctf)
    weight_other = to(weight_send, core_pairs)
    group_row = groups.astype(F32).reshape(1, count)
    group_row = jnp.concatenate([group_row, to(group_row, core_pairs)], axis=1).astype(jnp.int32)
    place = slots.T

    lane = jnp.arange(BW)
    freq_x = (lane % HALF + core * HALF - BW // 2).astype(F32)
    freq_y = jnp.arange(KB).astype(F32)
    shift_x = shifts[:, 0].astype(F32)
    shift_y = shifts[:, 1].astype(F32)
    angles = (
        2.0
        * math.pi
        / BW
        * (
            shift_x[None, :, None] * freq_x[None, None, :]
            + shift_y[None, :, None] * freq_y[:, None, None]
        )
    )
    cosine = jnp.cos(angles)
    sine = jnp.sin(angles) * jnp.where(lane < HALF, -1.0, 1.0)

    order = tuple(kz * ny + ky for kz, ky in pieces)
    (partial,) = call(
        functools.partial(score_kernel, order, rows),
        [SMEM] + [VMEM] * (6 + len(order)),
        [struct((shift_count * R, 2 * count), F32)],
        [
            pltpu.VMEM((chips * rows, BW), F32),
            pltpu.VMEM((GROUP, R, BW), F32),
            pltpu.VMEM((shift_count * R, GROUP * BW), BF16),
            pltpu.VMEM((2 * R, GROUP * BW), BF16),
            pltpu.VMEM((2 * R, 2 * ctf.shape[0]), F32),
        ],
        4 * 10**9,
        10**7,
        "score",
    )(target, group_row, cosine, sine, weight_keep, weight_other, squares, *pieces.values())

    theirs = to(partial, core_pairs)
    first = rows * 2 // 3
    later = rows - first
    outs = call(
        functools.partial(back_kernel, ny, nz, rows, first),
        [SMEM] + [VMEM] * 6,
        [struct((1, 2 * count), F32)]
        + [struct((nz * first, BW), BF16)] * ny
        + [struct((ny * later, BW), BF16)] * nz,
        [pltpu.VMEM((chips * rows, BW), F32), pltpu.VMEM((2, R, BW), F32)],
        4 * 10**9,
        10**7,
        "back",
    )(target, partial, theirs, cosine, sine, weight_keep, weight_other)
    evidence = outs[0][0, :count]
    by_y, by_z = outs[1 : 1 + ny], outs[1 + ny :]

    from_y = [to(by_y[ky], along_y(ky)) for ky in range(1, ny)]
    from_z = [to(by_z[kz], along_z(kz)) for kz in near]
    summed_y = by_y[0].astype(F32)
    for part in from_y:
        summed_y = summed_y + part.astype(F32)
    packed_y = summed_y.astype(BF16)
    final_first = summed_y[:first]
    for kz in near:
        part = to(packed_y[kz * first : (kz + 1) * first], along_z(kz))
        final_first = final_first + part.astype(F32)
    summed_z = by_z[0].astype(F32)
    for part in from_z:
        summed_z = summed_z + part.astype(F32)
    packed_z = summed_z.astype(BF16)
    final_later = summed_z[:later]
    for ky in range(1, ny):
        part = to(packed_z[ky * later : (ky + 1) * later], along_y(ky))
        final_later = final_later + part.astype(F32)
    final = jnp.concatenate([final_first, final_later], axis=0)
    sum_keep = final[:cap]
    sum_other = to(final[cap:], core_pairs)

    (new_map,) = call(
        adjoint_kernel,
        [SMEM] + [VMEM] * 6,
        [struct(volume.shape, F32)],
        [],
        10**9,
        2 * 10**6,
        "adjoint",
    )(meta, place, slots, volume, interp, sum_keep, sum_other)
    return (new_map, evidence)


def solution(mesh):
    return jax.shard_map(
        per_device,
        mesh=mesh,
        in_specs=(
            P(("parts", "img"), None),
            P(("parts", "img")),
            P("parts", None),
            P(("parts", "img"), None),
            P("parts", None),
            P("parts"),
            P("parts"),
            P(),
            P("parts", None),
        ),
        out_specs=(P(("parts", "img"), None), P(("parts", "img"))),
        check_vma=False,
    )
```

```python
import functools
import math

import jax
import jax.numpy as jnp
from jax import lax
from jax.experimental import pallas as pl
from jax.experimental.pallas import tpu as pltpu
from jax.sharding import PartitionSpec as P

BW = 128
KB = 64
R = 64
HALF = BW // 2
BLOCKS = R * KB
GROUP = 4

F32 = jnp.float32
BF16 = jnp.bfloat16
NT = (((1,), (1,)), ((), ()))
NN = (((1,), (0,)), ((), ()))


def dot(a, b, dims=NN):
    return lax.dot_general(a, b, dims, preferred_element_type=F32)


def iota(shape, axis):
    return lax.broadcasted_iota(jnp.int32, shape, axis)


def swap_halves(x):
    return pltpu.roll(x, HALF, 1)


def split_halves(real, imag):
    first = iota(real.shape, 1) < HALF
    return (
        jnp.where(first, real, swap_halves(imag)),
        jnp.where(first, swap_halves(real), imag),
    )


def triangles(rows):
    upper = jnp.where(iota((BW, BW), 0) <= iota((BW, BW), 1), 1.0, 0.0).astype(BF16)
    lower = jnp.where(iota((rows, rows), 1) < iota((rows, rows), 0), 1.0, 0.0).astype(BF16)
    return upper, jnp.ones((BW, BW), BF16), lower


def target_kernel(devices, ny, nz, cap, meta, owner, target):
    z, y, core = meta[1], meta[2], meta[3]
    own = owner[...]
    upper, ones, lower = triangles(own.shape[0])

    def rank(d, pos):
        member = jnp.where(own == d, 1.0, 0.0)
        bits = member.astype(BF16)
        before = dot(lower, dot(bits, ones).astype(BF16))
        return pos + member * (dot(bits, upper) - 1.0 + before)

    pos = jnp.zeros(own.shape, F32)
    if devices <= 16:
        for d in range(devices):
            pos = rank(d, pos)
    else:
        pos = lax.fori_loop(0, devices, rank, pos)
    rel_core = (own & 1) ^ core
    rel_y = (lax.shift_right_logical(own, 1) - y) & (ny - 1)
    rel_z = (lax.shift_right_logical(own, ny.bit_length()) - z) & (nz - 1)
    target[...] = ((rel_z * ny + rel_y) * 2 + rel_core) * cap + pos.astype(jnp.int32)


def slice_kernel(meta, *refs):
    sources, (slots, keep, send), held, arrived = refs[:5], refs[5:8], refs[8:13], refs[13]
    copies = [
        pltpu.make_async_copy(source, place, arrived.at[i])
        for i, (source, place) in enumerate(zip(sources, held))
    ]
    for copy in copies:
        copy.start()
    owner, local, table, volume, interp = held
    me, core = meta[0], meta[3]
    cap = keep.shape[0]
    for copy in copies[:3]:
        copy.wait()
    own = owner[...]
    rows = own.shape[0]
    upper, ones, lower = triangles(rows)
    member = own == me
    bits = jnp.where(member, 1.0, 0.0).astype(BF16)
    total = dot(bits, ones)
    before = dot(lower, total.astype(BF16))
    pos = (dot(bits, upper) - 1.0 + before).astype(jnp.int32)
    number = iota((rows, cap), 1).astype(F32)
    start, stop = before[:, 0:1], before[:, 0:1] + total[:, 0:1]
    row_hot = jnp.where(number >= start, jnp.where(number < stop, 1.0, 0.0), 0.0)
    loc = local[...]
    fields = [
        jnp.where(member, lax.shift_right_logical(pos, 7), 255),
        pos & 127,
        lax.shift_right_logical(loc, 8),
        loc & 255,
        table[...],
    ]
    fields = jnp.concatenate([f.astype(F32) for f in fields], axis=1).astype(BF16)
    found = dot(row_hot.T.astype(BF16), fields)
    slot = iota((cap, BW), 0).astype(F32)
    valid = slot < stop[rows - 1 : rows]
    hit = found[:, :BW] * 128.0 + found[:, BW : 2 * BW] == jnp.where(valid, slot, -1.0)
    place = jnp.where(hit, found[:, 2 * BW : 3 * BW] * 256.0 + found[:, 3 * BW : 4 * BW], 0.0)
    place = jnp.sum(place, axis=1, keepdims=True)
    place = jnp.where(valid[:, 0:1], place, -1.0)
    which = jnp.sum(jnp.where(hit, found[:, 4 * BW :], 0.0), axis=1, keepdims=True)
    column = iota((cap, 8), 1)
    slots[...] = jnp.where(column == 0, place, jnp.where(column == 1, which, 0.0))

    for copy in copies[3:]:
        copy.wait()
    depth = volume.shape[0]
    pick = jnp.where(iota((cap, depth), 1) == place.astype(jnp.int32), 1.0, 0.0).astype(BF16)
    voxels = dot(pick, volume[...])
    voxels = jnp.concatenate([voxels[:, :BW], voxels[:, BW:]], axis=0)
    which = jnp.concatenate([which, which], axis=0)
    out = jnp.zeros((2 * cap, BW), F32)
    for t in range(0, interp.shape[0], 2):
        pair = [jnp.where(which == float(t + i), voxels, 0.0).astype(BF16) for i in range(2)]
        out = out + dot(
            jnp.concatenate(pair, axis=1),
            jnp.concatenate([interp[t], interp[t + 1]], axis=1),
            NT,
        )
    left, right = split_halves(out[:cap], out[cap:])
    keep[...] = jnp.where(core == 0, left, right).astype(BF16)
    send[...] = jnp.where(core == 0, right, left).astype(BF16)


def weigh_kernel(meta, images, group, ctf, keep, send, squares):
    core = meta[3]
    count = images.shape[0]
    groups = ctf.shape[0]
    number = jnp.broadcast_to(group[...], (count, BW))

    def body(b, carry):
        lanes = pl.ds(pl.multiple_of(b * BW, BW), BW)
        scale = ctf[:, lanes]
        factor = jnp.zeros((count, BW), F32)
        for g in range(groups):
            factor = jnp.where(number == g, scale[g : g + 1], factor)
        real = images[:, pl.ds(pl.multiple_of(b * 2 * BW, BW), BW)].astype(F32) * factor
        imag = images[:, pl.ds(pl.multiple_of(b * 2 * BW + BW, BW), BW)].astype(F32) * factor
        left, right = split_halves(real, imag)
        keep[:, lanes] = jnp.where(core == 0, left, right).astype(BF16)
        send[:, lanes] = jnp.where(core == 0, right, left).astype(BF16)
        square = scale * scale
        left, right = split_halves(square, square)
        square = jnp.where(core == 0, left, right)
        high = square.astype(BF16)
        rest = square - high.astype(F32)
        squares[:, lanes] = jnp.concatenate([high.astype(F32), rest], axis=0).astype(BF16)
        return carry

    lax.fori_loop(0, KB, body, 0, unroll=2)


def score_kernel(
    places, target, group, cosine, sine, keep, other, squares, *rest
):
    pieces = rest[: len(places)]
    scores, gathered, norms, *stages = rest[len(places) :]
    blocks, lefts, powers = stages[0:2], stages[2:4], stages[4:6]
    shifts = cosine.shape[1]
    steps = KB // GROUP
    wide = GROUP * BW
    for piece, moves in zip(pieces, places):
        for source, size, start in moves:
            gathered[start + 8 : start + 8 + size, :] = piece[source : source + size, :].astype(F32)
    scores[...] = jnp.zeros(scores.shape, F32)
    norms[...] = jnp.zeros(norms.shape, F32)

    sublane = iota((8, BW), 0)

    def fetch(b, first):
        value = None
        for k in range(8):
            row = target[(first + k) * KB + b]
            loaded = gathered[pl.ds(row - k + 8, 8), :]
            value = loaded if k == 0 else jnp.where(sublane == k, loaded, value)
        return value

    def gather(step, block):
        for part in range(GROUP):
            for first in range(0, R, 8):
                block[part, first : first + 8, :] = fetch(step * GROUP + part, first)

    def rotate(step, block, left, power):
        for part in range(GROUP):
            b = step * GROUP + part
            lanes = slice(part * BW, (part + 1) * BW)
            value = block[part]
            swapped = swap_halves(value)
            for s in range(shifts):
                turned = value * cosine[b, s : s + 1, :] + swapped * sine[b, s : s + 1, :]
                left[s * R : (s + 1) * R, lanes] = turned.astype(BF16)
            square = value * value
            high = square.astype(BF16)
            power[0:R, lanes] = high
            power[R : 2 * R, lanes] = (square - high.astype(F32)).astype(BF16)

    def multiply(step, left, power):
        lanes = pl.ds(pl.multiple_of(step * wide, wide), wide)
        right = jnp.concatenate([keep[:, lanes], other[:, lanes]], axis=0)
        scores[...] += dot(left[...], right, NT)
        norms[...] += dot(power[...], squares[:, lanes], NT)

    def body(pair, carry):
        for half in range(2):
            step = 2 * pair + half
            gather(jnp.minimum(step + 1, steps - 1), blocks[1 - half])
            rotate(step, blocks[half], lefts[half], powers[half])
            multiply(jnp.maximum(step - 1, 0), lefts[1 - half], powers[1 - half])
        return carry

    gather(0, blocks[0])
    lefts[1][...] = jnp.zeros(lefts[1].shape, BF16)
    powers[1][...] = jnp.zeros(powers[1].shape, BF16)
    lax.fori_loop(0, steps // 2, body, 0)
    multiply(steps - 1, lefts[1], powers[1])
    half = squares.shape[0] // 2
    total = norms[...]
    total = total[:R, :half] + total[:R, half:] + total[R:, :half] + total[R:, half:]
    norm = jnp.zeros((R, scores.shape[1]), F32)
    for g in range(half):
        norm = jnp.where(group[...] == g, total[:, g : g + 1], norm)
    for s in range(shifts):
        scores[s * R : (s + 1) * R, :] -= 0.5 * norm


def back_kernel(ny, nz, rows, first, target, mine, theirs, cosine, sine, keep, other, *rest):
    evidence = rest[0]
    parts = rest[1 : 1 + ny * nz]
    by_z = rest[1 + ny * nz : 1 + ny * nz + nz]
    (placed,) = rest[1 + ny * nz + nz :]
    shifts = cosine.shape[1]
    scale = 1.0 / math.sqrt(KB * BW)
    placed[...] = jnp.zeros(placed.shape, F32)
    scores = (mine[...] + swap_halves(theirs[...])) * scale
    top = jnp.max(scores, axis=0, keepdims=True)
    exponent = jnp.exp(scores - top)
    total = jnp.sum(exponent, axis=0, keepdims=True)
    evidence[...] = top + jnp.log(total)
    weights = (exponent / total).astype(BF16)
    sublane = iota((8, BW), 0)

    def body(pair, carry):
        lanes = pl.ds(pl.multiple_of(pair * 2 * BW, BW), 2 * BW)
        right = jnp.concatenate([keep[:, lanes], other[:, lanes]], axis=0)
        sums = dot(weights, right)
        for part in range(2):
            b = pair * 2 + part
            straight = jnp.zeros((R, BW), F32)
            crossed = jnp.zeros((R, BW), F32)
            for s in range(shifts):
                term = sums[s * R : (s + 1) * R, part * BW : (part + 1) * BW]
                straight = straight + term * cosine[b, s : s + 1, :]
                crossed = crossed + term * sine[b, s : s + 1, :]
            value = straight + swap_halves(crossed)
            for r in range(R):
                k = r % 8
                row = target[r * KB + b]
                pltpu.store(
                    placed.at[pl.ds(row + (8 - k), 8), :],
                    value[r - k : r - k + 8],
                    mask=sublane == k,
                )
        return carry

    lax.fori_loop(0, KB // 2, body, 0, unroll=4)
    later = rows - first
    for kz in range(nz):
        for ky in range(ny):
            start = (kz * ny + ky) * rows + 8
            parts[kz * ny + ky][...] = placed[start : start + first, :].astype(BF16)
            by_z[kz][ky * later : (ky + 1) * later, :] = placed[
                start + first : start + rows, :
            ].astype(BF16)


def adjoint_kernel(meta, place, slots, volume, interp, keep, other, new_map):
    core = meta[3]
    cap = keep.shape[0]
    mine, theirs = keep[...], other[...]
    left = jnp.where(core == 0, mine, theirs)
    right = jnp.where(core == 0, theirs, mine)
    real, imag = split_halves(left, right)
    value = jnp.concatenate([real, imag], axis=0)
    which = slots[:, 1:2]
    which = jnp.concatenate([which, which], axis=0)
    high = value.astype(BF16).astype(F32)
    rest = value - high
    out = jnp.zeros((2 * cap, BW), F32)
    for t in range(0, interp.shape[0], 2):
        matrix = jnp.concatenate([interp[t], interp[t + 1]], axis=0)
        for part in (high, rest):
            pair = [jnp.where(which == float(t + i), part, 0.0).astype(BF16) for i in range(2)]
            out = out + dot(jnp.concatenate(pair, axis=1), matrix)
    out = jnp.concatenate([out[:cap], out[cap:]], axis=1)
    depth = volume.shape[0]
    spread = jnp.where(
        iota((depth, cap), 0) == place[0:1, :].astype(jnp.int32), 1.0, 0.0
    ).astype(BF16)
    high = out.astype(BF16)
    rest = (out - high.astype(F32)).astype(BF16)
    new_map[...] = volume[...].astype(F32) + (dot(spread, high) + dot(spread, rest))


SMEM = pl.BlockSpec(memory_space=pltpu.SMEM)
VMEM = pl.BlockSpec(memory_space=pltpu.VMEM)
ANY = pl.BlockSpec(memory_space=pl.ANY)


def call(kernel, in_specs, out_shapes, scratch, flops, touched, name, limit=40):
    return pl.pallas_call(
        kernel,
        in_specs=in_specs,
        out_specs=[VMEM] * len(out_shapes),
        out_shape=out_shapes,
        scratch_shapes=scratch,
        compiler_params=pltpu.CompilerParams(vmem_limit_bytes=limit * 1024 * 1024),
        cost_estimate=pl.CostEstimate(flops=flops, bytes_accessed=touched, transcendentals=0),
        name=name,
    )


def per_device(images, groups, shifts, volume, owner, local, table_id, interp, ctf):
    devices = lax.axis_size("img")
    chips = devices // 2
    ny = 1 << ((chips.bit_length() - 1) // 2)
    nz = chips // ny
    me = lax.axis_index("img")
    core = me % 2
    y = (me // 2) % ny
    z = me // (2 * ny)
    meta = jnp.stack([me, z, y, core]).astype(jnp.int32)
    cap = max(2, 3 * BLOCKS // (2 * devices))
    rows = 2 * cap
    count = images.shape[0]
    shift_count = shifts.shape[0]
    struct = jax.ShapeDtypeStruct

    def device(dz, dy, dc):
        return (dz * ny + dy) * 2 + dc

    everyone = [(dz, dy, dc) for dz in range(nz) for dy in range(ny) for dc in range(2)]
    core_pairs = [(device(*d), device(d[0], d[1], 1 - d[2])) for d in everyone]

    def along_z(k):
        return [(device(a, b, c), device((a + k) % nz, b, c)) for a, b, c in everyone]

    def along_y(k):
        return [(device(a, b, c), device(a, (b + k) % ny, c)) for a, b, c in everyone]

    def to(array, pairs):
        return lax.ppermute(array, "img", pairs)

    wide = (BLOCKS // BW, BW)
    owner = owner.reshape(wide)
    slots, slice_keep, slice_send = call(
        slice_kernel,
        [SMEM] + [ANY] * 5,
        [struct((cap, 8), F32), struct((cap, BW), BF16), struct((cap, BW), BF16)],
        [pltpu.VMEM(wide, jnp.int32)] * 3
        + [
            pltpu.VMEM(volume.shape, BF16),
            pltpu.VMEM(interp.shape, BF16),
            pltpu.SemaphoreType.DMA((5,)),
        ],
        10**9,
        10**6,
        "own_slices",
        60,
    )(meta, owner, local.reshape(wide), table_id.reshape(wide), volume, interp)
    own_piece = jnp.concatenate([slice_keep, to(slice_send, core_pairs)], axis=0)
    images, owner, groups, shifts, _ = lax.optimization_barrier(
        (images, owner, groups, shifts, own_piece)
    )
    (target,) = call(
        functools.partial(target_kernel, devices, ny, nz, cap),
        [SMEM, VMEM],
        [struct(wide, jnp.int32)],
        [],
        10**9,
        10**6,
        "target",
    )(meta, owner)
    target = target.reshape(BLOCKS)

    later = max(16, rows // 6 // 16 * 16)
    first = rows - later
    near = sorted(range(1, nz), key=lambda k: min(k, nz - k))
    pieces = [(own_piece, [(0, rows, 0)])]
    others = [own_piece[first:]]
    by_z = {kz: to(own_piece[:first], along_z(-kz)) for kz in near}
    for ky in range(1, ny):
        piece = to(own_piece, along_y(-ky))
        pieces.append((piece, [(0, rows, ky * rows)]))
        others.append(piece[first:])
    others = jnp.concatenate(others, axis=0)
    for kz in near:
        start = kz * ny * rows
        pieces.append((by_z[kz], [(0, first, start)]))
        for ky in range(1, ny):
            piece = to(by_z[kz], along_y(-ky))
            pieces.append((piece, [(0, first, start + ky * rows)]))
    for kz in near:
        start = kz * ny * rows + first
        piece = to(others, along_z(-kz))
        pieces.append((piece, [(ky * later, later, start + ky * rows) for ky in range(ny)]))

    weight_keep, weight_send, squares = call(
        weigh_kernel,
        [SMEM] + [VMEM] * 3,
        [
            struct((count, KB * BW), BF16),
            struct((count, KB * BW), BF16),
            struct((2 * ctf.shape[0], KB * BW), BF16),
        ],
        [],
        10**9,
        4 * 10**6,
        "weigh",
    )(meta, images, groups.reshape(count, 1), ctf)
    weight_other = to(weight_send, core_pairs)
    group_row = groups.astype(F32).reshape(1, count)
    group_row = jnp.concatenate([group_row, to(group_row, core_pairs)], axis=1).astype(jnp.int32)
    place = slots.T

    lane = jnp.arange(BW)
    freq_x = (lane % HALF + core * HALF - BW // 2).astype(F32)
    freq_y = jnp.arange(KB).astype(F32)
    shift_x = shifts[:, 0].astype(F32)
    shift_y = shifts[:, 1].astype(F32)
    angles = (
        2.0
        * math.pi
        / BW
        * (
            shift_x[None, :, None] * freq_x[None, None, :]
            + shift_y[None, :, None] * freq_y[:, None, None]
        )
    )
    cosine = jnp.cos(angles)
    sine = jnp.sin(angles) * jnp.where(lane < HALF, -1.0, 1.0)

    (partial,) = call(
        functools.partial(score_kernel, [moves for _, moves in pieces]),
        [SMEM] + [VMEM] * (6 + len(pieces)),
        [struct((shift_count * R, 2 * count), F32)],
        [
            pltpu.VMEM((chips * rows + 16, BW), F32),
            pltpu.VMEM((2 * R, 2 * ctf.shape[0]), F32),
        ]
        + [pltpu.VMEM((GROUP, R, BW), F32)] * 2
        + [pltpu.VMEM((shift_count * R, GROUP * BW), BF16)] * 2
        + [pltpu.VMEM((2 * R, GROUP * BW), BF16)] * 2,
        4 * 10**9,
        10**7,
        "score",
    )(target, group_row, cosine, sine, weight_keep, weight_other, squares, *[piece for piece, _ in pieces])

    theirs = to(partial, core_pairs)
    outs = call(
        functools.partial(back_kernel, ny, nz, rows, first),
        [SMEM] + [VMEM] * 6,
        [struct((1, 2 * count), F32)]
        + [struct((first, BW), BF16)] * chips
        + [struct((ny * later, BW), BF16)] * nz,
        [pltpu.VMEM((chips * rows + 16, BW), F32)],
        4 * 10**9,
        10**7,
        "back",
    )(target, partial, theirs, cosine, sine, weight_keep, weight_other)
    evidence = outs[0][0, :count]
    parts, by_z = outs[1 : 1 + chips], outs[1 + chips :]

    far = near[::-1]
    summed = {}
    from_y = {}
    for kz in far + [0]:
        from_y[kz] = [to(parts[kz * ny + ky], along_y(ky)) for ky in range(1, ny)]
    from_z = [to(by_z[kz], along_z(kz)) for kz in far]
    for kz in far + [0]:
        summed[kz] = parts[kz * ny].astype(F32)
        for part in from_y[kz]:
            summed[kz] = summed[kz] + part.astype(F32)
    final_first = summed[0]
    for kz in far:
        final_first = final_first + to(summed[kz].astype(BF16), along_z(kz)).astype(F32)
    summed_z = by_z[0].astype(F32)
    for part in from_z:
        summed_z = summed_z + part.astype(F32)
    packed_z = summed_z.astype(BF16)
    final_later = summed_z[:later]
    for ky in range(1, ny):
        part = to(packed_z[ky * later : (ky + 1) * later], along_y(ky))
        final_later = final_later + part.astype(F32)
    final = jnp.concatenate([final_first, final_later], axis=0)
    sum_keep = final[:cap]
    sum_other = to(final[cap:], core_pairs)

    (new_map,) = call(
        adjoint_kernel,
        [SMEM] + [VMEM] * 6,
        [struct(volume.shape, F32)],
        [],
        10**9,
        2 * 10**6,
        "adjoint",
    )(meta, place, slots, volume, interp, sum_keep, sum_other)
    return (new_map, evidence)


def solution(mesh):
    return jax.shard_map(
        per_device,
        mesh=mesh,
        in_specs=(
            P(("parts", "img"), None),
            P(("parts", "img")),
            P("parts", None),
            P(("parts", "img"), None),
            P("parts", None),
            P("parts"),
            P("parts"),
            P(),
            P("parts", None),
        ),
        out_specs=(P(("parts", "img"), None), P(("parts", "img"))),
        check_vma=False,
    )
```

```python
import functools
import math

import jax
import jax.numpy as jnp
from jax import lax
from jax.experimental import pallas as pl
from jax.experimental.pallas import tpu as pltpu
from jax.sharding import PartitionSpec as P

BW = 128
KB = 64
R = 64
HALF = BW // 2
BLOCKS = R * KB
GROUP = 4

F32 = jnp.float32
BF16 = jnp.bfloat16
NT = (((1,), (1,)), ((), ()))
NN = (((1,), (0,)), ((), ()))


def dot(a, b, dims=NN):
    return lax.dot_general(a, b, dims, preferred_element_type=F32)


def iota(shape, axis):
    return lax.broadcasted_iota(jnp.int32, shape, axis)


def swap_halves(x):
    return pltpu.roll(x, HALF, 1)


def split_halves(real, imag):
    first = iota(real.shape, 1) < HALF
    return (
        jnp.where(first, real, swap_halves(imag)),
        jnp.where(first, swap_halves(real), imag),
    )


def triangles(rows):
    upper = jnp.where(iota((BW, BW), 0) <= iota((BW, BW), 1), 1.0, 0.0).astype(BF16)
    lower = jnp.where(iota((rows, rows), 1) < iota((rows, rows), 0), 1.0, 0.0).astype(BF16)
    return upper, jnp.ones((BW, BW), BF16), lower


def target_kernel(devices, ny, nz, cap, meta, owner, target):
    z, y, core = meta[1], meta[2], meta[3]
    own = owner[...]
    upper, ones, lower = triangles(own.shape[0])

    def rank(d, pos):
        member = jnp.where(own == d, 1.0, 0.0)
        bits = member.astype(BF16)
        before = dot(lower, dot(bits, ones).astype(BF16))
        return pos + member * (dot(bits, upper) - 1.0 + before)

    pos = jnp.zeros(own.shape, F32)
    if devices <= 16:
        for d in range(devices):
            pos = rank(d, pos)
    else:
        pos = lax.fori_loop(0, devices, rank, pos)
    rel_core = (own & 1) ^ core
    rel_y = (lax.shift_right_logical(own, 1) - y) & (ny - 1)
    rel_z = (lax.shift_right_logical(own, ny.bit_length()) - z) & (nz - 1)
    target[...] = ((rel_z * ny + rel_y) * 2 + rel_core) * cap + pos.astype(jnp.int32)


def slice_kernel(meta, *refs):
    sources, (slots, keep, send), held, arrived = refs[:5], refs[5:8], refs[8:13], refs[13]
    copies = [
        pltpu.make_async_copy(source, place, arrived.at[i])
        for i, (source, place) in enumerate(zip(sources, held))
    ]
    for copy in copies:
        copy.start()
    owner, local, table, volume, interp = held
    me, core = meta[0], meta[3]
    cap = keep.shape[0]
    for copy in copies[:3]:
        copy.wait()
    own = owner[...]
    rows = own.shape[0]
    upper, ones, lower = triangles(rows)
    member = own == me
    bits = jnp.where(member, 1.0, 0.0).astype(BF16)
    total = dot(bits, ones)
    before = dot(lower, total.astype(BF16))
    pos = (dot(bits, upper) - 1.0 + before).astype(jnp.int32)
    number = iota((rows, cap), 1).astype(F32)
    start, stop = before[:, 0:1], before[:, 0:1] + total[:, 0:1]
    row_hot = jnp.where(number >= start, jnp.where(number < stop, 1.0, 0.0), 0.0)
    loc = local[...]
    fields = [
        jnp.where(member, lax.shift_right_logical(pos, 7), 255),
        pos & 127,
        lax.shift_right_logical(loc, 8),
        loc & 255,
        table[...],
    ]
    fields = jnp.concatenate([f.astype(F32) for f in fields], axis=1).astype(BF16)
    found = dot(row_hot.T.astype(BF16), fields)
    slot = iota((cap, BW), 0).astype(F32)
    valid = slot < stop[rows - 1 : rows]
    hit = found[:, :BW] * 128.0 + found[:, BW : 2 * BW] == jnp.where(valid, slot, -1.0)
    place = jnp.where(hit, found[:, 2 * BW : 3 * BW] * 256.0 + found[:, 3 * BW : 4 * BW], 0.0)
    place = jnp.sum(place, axis=1, keepdims=True)
    place = jnp.where(valid[:, 0:1], place, -1.0)
    which = jnp.sum(jnp.where(hit, found[:, 4 * BW :], 0.0), axis=1, keepdims=True)
    column = iota((cap, 8), 1)
    slots[...] = jnp.where(column == 0, place, jnp.where(column == 1, which, 0.0))

    for copy in copies[3:]:
        copy.wait()
    depth = volume.shape[0]
    pick = jnp.where(iota((cap, depth), 1) == place.astype(jnp.int32), 1.0, 0.0).astype(BF16)
    voxels = dot(pick, volume[...])
    voxels = jnp.concatenate([voxels[:, :BW], voxels[:, BW:]], axis=0)
    which = jnp.concatenate([which, which], axis=0)
    tables = range(interp.shape[0])
    chosen = [jnp.where(which == float(t), voxels, 0.0).astype(BF16) for t in tables]
    matrix = jnp.concatenate([interp[t] for t in tables], axis=1)
    out = dot(jnp.concatenate(chosen, axis=1), matrix, NT)
    left, right = split_halves(out[:cap], out[cap:])
    keep[...] = jnp.where(core == 0, left, right).astype(BF16)
    send[...] = jnp.where(core == 0, right, left).astype(BF16)


def weigh_kernel(meta, images, group, ctf, keep, send, squares):
    core = meta[3]
    count = images.shape[0]
    groups = ctf.shape[0]
    number = jnp.broadcast_to(group[...], (count, BW))

    def body(b, carry):
        lanes = pl.ds(pl.multiple_of(b * BW, BW), BW)
        scale = ctf[:, lanes]
        factor = jnp.zeros((count, BW), F32)
        for g in range(groups):
            factor = jnp.where(number == g, scale[g : g + 1], factor)
        real = images[:, pl.ds(pl.multiple_of(b * 2 * BW, BW), BW)].astype(F32) * factor
        imag = images[:, pl.ds(pl.multiple_of(b * 2 * BW + BW, BW), BW)].astype(F32) * factor
        left, right = split_halves(real, imag)
        keep[:, lanes] = jnp.where(core == 0, left, right).astype(BF16)
        send[:, lanes] = jnp.where(core == 0, right, left).astype(BF16)
        square = scale * scale
        left, right = split_halves(square, square)
        square = jnp.where(core == 0, left, right)
        high = square.astype(BF16)
        rest = square - high.astype(F32)
        squares[:, lanes] = jnp.concatenate([high.astype(F32), rest], axis=0).astype(BF16)
        return carry

    lax.fori_loop(0, KB, body, 0, unroll=8)


def score_kernel(
    places, target, group, cosine, sine, keep, other, squares, *rest
):
    pieces = rest[: len(places)]
    scores, gathered, norms, *stages = rest[len(places) :]
    blocks, lefts, powers = stages[0:2], stages[2:4], stages[4:6]
    shifts = cosine.shape[1]
    steps = KB // GROUP
    wide = GROUP * BW
    for piece, moves in zip(pieces, places):
        for source, size, start in moves:
            gathered[start + 8 : start + 8 + size, :] = piece[source : source + size, :].astype(F32)
    scores[...] = jnp.zeros(scores.shape, F32)
    norms[...] = jnp.zeros(norms.shape, F32)

    sublane = iota((8, BW), 0)

    def fetch(b, first):
        value = None
        for k in range(8):
            row = target[(first + k) * KB + b]
            loaded = gathered[pl.ds(row - k + 8, 8), :]
            value = loaded if k == 0 else jnp.where(sublane == k, loaded, value)
        return value

    def gather(step, block):
        for part in range(GROUP):
            for first in range(0, R, 8):
                block[part, first : first + 8, :] = fetch(step * GROUP + part, first)

    def rotate(step, block, left, power):
        for part in range(GROUP):
            b = step * GROUP + part
            lanes = slice(part * BW, (part + 1) * BW)
            value = block[part]
            swapped = swap_halves(value)
            for s in range(shifts):
                turned = value * cosine[b, s : s + 1, :] + swapped * sine[b, s : s + 1, :]
                left[s * R : (s + 1) * R, lanes] = turned.astype(BF16)
            square = value * value
            high = square.astype(BF16)
            power[0:R, lanes] = high
            power[R : 2 * R, lanes] = (square - high.astype(F32)).astype(BF16)

    def multiply(step, left, power):
        lanes = pl.ds(pl.multiple_of(step * wide, wide), wide)
        right = jnp.concatenate([keep[:, lanes], other[:, lanes]], axis=0)
        scores[...] += dot(left[...], right, NT)
        norms[...] += dot(power[...], squares[:, lanes], NT)

    def body(pair, carry):
        for half in range(2):
            step = 2 * pair + half
            gather(jnp.minimum(step + 1, steps - 1), blocks[1 - half])
            rotate(step, blocks[half], lefts[half], powers[half])
            multiply(jnp.maximum(step - 1, 0), lefts[1 - half], powers[1 - half])
        return carry

    gather(0, blocks[0])
    lefts[1][...] = jnp.zeros(lefts[1].shape, BF16)
    powers[1][...] = jnp.zeros(powers[1].shape, BF16)
    lax.fori_loop(0, steps // 2, body, 0)
    multiply(steps - 1, lefts[1], powers[1])
    half = squares.shape[0] // 2
    total = norms[...]
    total = total[:R, :half] + total[:R, half:] + total[R:, :half] + total[R:, half:]
    norm = jnp.zeros((R, scores.shape[1]), F32)
    for g in range(half):
        norm = jnp.where(group[...] == g, total[:, g : g + 1], norm)
    for s in range(shifts):
        scores[s * R : (s + 1) * R, :] -= 0.5 * norm


def back_kernel(ny, nz, rows, first, target, mine, theirs, cosine, sine, keep, other, *rest):
    evidence = rest[0]
    parts = rest[1 : 1 + ny * nz]
    by_z = rest[1 + ny * nz : 1 + ny * nz + nz]
    (placed,) = rest[1 + ny * nz + nz :]
    shifts = cosine.shape[1]
    scale = 1.0 / math.sqrt(KB * BW)
    placed[...] = jnp.zeros(placed.shape, F32)
    scores = (mine[...] + swap_halves(theirs[...])) * scale
    top = jnp.max(scores, axis=0, keepdims=True)
    exponent = jnp.exp(scores - top)
    total = jnp.sum(exponent, axis=0, keepdims=True)
    evidence[...] = top + jnp.log(total)
    weights = (exponent / total).astype(BF16)
    sublane = iota((8, BW), 0)

    def body(pair, carry):
        lanes = pl.ds(pl.multiple_of(pair * 2 * BW, BW), 2 * BW)
        right = jnp.concatenate([keep[:, lanes], other[:, lanes]], axis=0)
        sums = dot(weights, right)
        for part in range(2):
            b = pair * 2 + part
            straight = jnp.zeros((R, BW), F32)
            crossed = jnp.zeros((R, BW), F32)
            for s in range(shifts):
                term = sums[s * R : (s + 1) * R, part * BW : (part + 1) * BW]
                straight = straight + term * cosine[b, s : s + 1, :]
                crossed = crossed + term * sine[b, s : s + 1, :]
            value = straight + swap_halves(crossed)
            for r in range(R):
                k = r % 8
                row = target[r * KB + b]
                pltpu.store(
                    placed.at[pl.ds(row + (8 - k), 8), :],
                    value[r - k : r - k + 8],
                    mask=sublane == k,
                )
        return carry

    lax.fori_loop(0, KB // 2, body, 0, unroll=4)
    later = rows - first
    for kz in range(nz):
        for ky in range(ny):
            start = (kz * ny + ky) * rows + 8
            parts[kz * ny + ky][...] = placed[start : start + first, :].astype(BF16)
            by_z[kz][ky * later : (ky + 1) * later, :] = placed[
                start + first : start + rows, :
            ].astype(BF16)


def adjoint_kernel(meta, place, slots, volume, interp, keep, other, new_map):
    core = meta[3]
    cap = keep.shape[0]
    mine, theirs = keep[...], other[...]
    left = jnp.where(core == 0, mine, theirs)
    right = jnp.where(core == 0, theirs, mine)
    real, imag = split_halves(left, right)
    value = jnp.concatenate([real, imag], axis=0)
    which = slots[:, 1:2]
    which = jnp.concatenate([which, which], axis=0)
    tables = range(interp.shape[0])
    matrix = jnp.concatenate([interp[t] for t in tables], axis=0)
    high = value.astype(BF16).astype(F32)
    out = jnp.zeros((2 * cap, BW), F32)
    for part in (high, value - high):
        chosen = [jnp.where(which == float(t), part, 0.0).astype(BF16) for t in tables]
        out = out + dot(jnp.concatenate(chosen, axis=1), matrix)
    out = jnp.concatenate([out[:cap], out[cap:]], axis=1)
    depth = volume.shape[0]
    spread = jnp.where(
        iota((depth, cap), 0) == place[0:1, :].astype(jnp.int32), 1.0, 0.0
    ).astype(BF16)
    high = out.astype(BF16)
    rest = (out - high.astype(F32)).astype(BF16)
    new_map[...] = volume[...].astype(F32) + dot(
        jnp.concatenate([spread, spread], axis=1), jnp.concatenate([high, rest], axis=0)
    )


SMEM = pl.BlockSpec(memory_space=pltpu.SMEM)
VMEM = pl.BlockSpec(memory_space=pltpu.VMEM)
ANY = pl.BlockSpec(memory_space=pl.ANY)


def call(kernel, in_specs, out_shapes, scratch, flops, touched, name, limit=40):
    return pl.pallas_call(
        kernel,
        in_specs=in_specs,
        out_specs=[VMEM] * len(out_shapes),
        out_shape=out_shapes,
        scratch_shapes=scratch,
        compiler_params=pltpu.CompilerParams(vmem_limit_bytes=limit * 1024 * 1024),
        cost_estimate=pl.CostEstimate(flops=flops, bytes_accessed=touched, transcendentals=0),
        name=name,
    )


def per_device(images, groups, shifts, volume, owner, local, table_id, interp, ctf):
    devices = lax.axis_size("img")
    chips = devices // 2
    ny = 1 << ((chips.bit_length() - 1) // 2)
    nz = chips // ny
    me = lax.axis_index("img")
    core = me % 2
    y = (me // 2) % ny
    z = me // (2 * ny)
    meta = jnp.stack([me, z, y, core]).astype(jnp.int32)
    cap = max(2, 3 * BLOCKS // (2 * devices))
    rows = 2 * cap
    count = images.shape[0]
    shift_count = shifts.shape[0]
    struct = jax.ShapeDtypeStruct

    def device(dz, dy, dc):
        return (dz * ny + dy) * 2 + dc

    everyone = [(dz, dy, dc) for dz in range(nz) for dy in range(ny) for dc in range(2)]
    core_pairs = [(device(*d), device(d[0], d[1], 1 - d[2])) for d in everyone]

    def along_z(k):
        return [(device(a, b, c), device((a + k) % nz, b, c)) for a, b, c in everyone]

    def along_y(k):
        return [(device(a, b, c), device(a, (b + k) % ny, c)) for a, b, c in everyone]

    def to(array, pairs):
        return lax.ppermute(array, "img", pairs)

    wide = (BLOCKS // BW, BW)
    owner = owner.reshape(wide)
    slots, slice_keep, slice_send = call(
        slice_kernel,
        [SMEM] + [ANY] * 5,
        [struct((cap, 8), F32), struct((cap, BW), BF16), struct((cap, BW), BF16)],
        [pltpu.VMEM(wide, jnp.int32)] * 3
        + [
            pltpu.VMEM(volume.shape, BF16),
            pltpu.VMEM(interp.shape, BF16),
            pltpu.SemaphoreType.DMA((5,)),
        ],
        10**9,
        10**6,
        "own_slices",
        60,
    )(meta, owner, local.reshape(wide), table_id.reshape(wide), volume, interp)
    own_piece = jnp.concatenate([slice_keep, to(slice_send, core_pairs)], axis=0)
    images, groups, _ = lax.optimization_barrier((images, groups, own_piece))

    later = max(16, rows // 6 // 16 * 16)
    first = rows - later
    near = sorted(range(1, nz), key=lambda k: min(k, nz - k))
    pieces = [(own_piece, [(0, rows, 0)])]
    by_z = {kz: to(own_piece, along_z(-kz)) for kz in near}
    for ky in range(1, ny):
        pieces.append((to(own_piece, along_y(-ky)), [(0, rows, ky * rows)]))
    for kz in near:
        start = kz * ny * rows
        pieces.append((by_z[kz], [(0, rows, start)]))
        for ky in range(1, ny):
            piece = to(by_z[kz], along_y(-ky))
            pieces.append((piece, [(0, rows, start + ky * rows)]))

    owner, shifts, _ = lax.optimization_barrier((owner, shifts, by_z[near[0]]))
    (target,) = call(
        functools.partial(target_kernel, devices, ny, nz, cap),
        [SMEM, VMEM],
        [struct(wide, jnp.int32)],
        [],
        10**9,
        10**6,
        "target",
    )(meta, owner)
    target = target.reshape(BLOCKS)

    weight_keep, weight_send, squares = call(
        weigh_kernel,
        [SMEM] + [VMEM] * 3,
        [
            struct((count, KB * BW), BF16),
            struct((count, KB * BW), BF16),
            struct((2 * ctf.shape[0], KB * BW), BF16),
        ],
        [],
        10**9,
        4 * 10**6,
        "weigh",
    )(meta, images, groups.reshape(count, 1), ctf)
    weight_other = to(weight_send, core_pairs)
    group_row = groups.astype(F32).reshape(1, count)
    group_row = jnp.concatenate([group_row, to(group_row, core_pairs)], axis=1).astype(jnp.int32)
    place = slots.T

    lane = jnp.arange(BW)
    freq_x = (lane % HALF + core * HALF - BW // 2).astype(F32)
    freq_y = jnp.arange(KB).astype(F32)
    shift_x = shifts[:, 0].astype(F32)
    shift_y = shifts[:, 1].astype(F32)
    angles = (
        2.0
        * math.pi
        / BW
        * (
            shift_x[None, :, None] * freq_x[None, None, :]
            + shift_y[None, :, None] * freq_y[:, None, None]
        )
    )
    cosine = jnp.cos(angles)
    sine = jnp.sin(angles) * jnp.where(lane < HALF, -1.0, 1.0)

    (partial,) = call(
        functools.partial(score_kernel, [moves for _, moves in pieces]),
        [SMEM] + [VMEM] * (6 + len(pieces)),
        [struct((shift_count * R, 2 * count), F32)],
        [
            pltpu.VMEM((chips * rows + 16, BW), F32),
            pltpu.VMEM((2 * R, 2 * ctf.shape[0]), F32),
        ]
        + [pltpu.VMEM((GROUP, R, BW), F32)] * 2
        + [pltpu.VMEM((shift_count * R, GROUP * BW), BF16)] * 2
        + [pltpu.VMEM((2 * R, GROUP * BW), BF16)] * 2,
        4 * 10**9,
        10**7,
        "score",
    )(target, group_row, cosine, sine, weight_keep, weight_other, squares, *[piece for piece, _ in pieces])

    theirs = to(partial, core_pairs)
    outs = call(
        functools.partial(back_kernel, ny, nz, rows, first),
        [SMEM] + [VMEM] * 6,
        [struct((1, 2 * count), F32)]
        + [struct((first, BW), BF16)] * chips
        + [struct((ny * later, BW), BF16)] * nz,
        [pltpu.VMEM((chips * rows + 16, BW), F32)],
        4 * 10**9,
        10**7,
        "back",
    )(target, partial, theirs, cosine, sine, weight_keep, weight_other)
    evidence = outs[0][0, :count]
    parts, by_z = outs[1 : 1 + chips], outs[1 + chips :]

    far = near[::-1]
    summed = {}
    from_y = {}
    for kz in far + [0]:
        from_y[kz] = [to(parts[kz * ny + ky], along_y(ky)) for ky in range(1, ny)]
    from_z = [to(by_z[kz], along_z(kz)) for kz in far]
    for kz in far + [0]:
        summed[kz] = parts[kz * ny].astype(F32)
        for part in from_y[kz]:
            summed[kz] = summed[kz] + part.astype(F32)
    final_first = summed[0]
    for kz in far:
        final_first = final_first + to(summed[kz].astype(BF16), along_z(kz)).astype(F32)
    summed_z = by_z[0].astype(F32)
    for part in from_z:
        summed_z = summed_z + part.astype(F32)
    packed_z = summed_z.astype(BF16)
    final_later = summed_z[:later]
    for ky in range(1, ny):
        part = to(packed_z[ky * later : (ky + 1) * later], along_y(ky))
        final_later = final_later + part.astype(F32)
    final = jnp.concatenate([final_first, final_later], axis=0)
    sum_keep = final[:cap]
    sum_other = to(final[cap:], core_pairs)

    (new_map,) = call(
        adjoint_kernel,
        [SMEM] + [VMEM] * 6,
        [struct(volume.shape, F32)],
        [],
        10**9,
        2 * 10**6,
        "adjoint",
    )(meta, place, slots, volume, interp, sum_keep, sum_other)
    return (new_map, evidence)


def solution(mesh):
    return jax.shard_map(
        per_device,
        mesh=mesh,
        in_specs=(
            P(("parts", "img"), None),
            P(("parts", "img")),
            P("parts", None),
            P(("parts", "img"), None),
            P("parts", None),
            P("parts"),
            P("parts"),
            P(),
            P("parts", None),
        ),
        out_specs=(P(("parts", "img"), None), P(("parts", "img"))),
        check_vma=False,
    )
```

```python
import functools
import math

import jax
import jax.numpy as jnp
from jax import lax
from jax.experimental import pallas as pl
from jax.experimental.pallas import tpu as pltpu
from jax.sharding import PartitionSpec as P

BW = 128
KB = 64
R = 64
HALF = BW // 2
BLOCKS = R * KB
GROUP = 4

F32 = jnp.float32
BF16 = jnp.bfloat16
NT = (((1,), (1,)), ((), ()))
NN = (((1,), (0,)), ((), ()))


def dot(a, b, dims=NN):
    return lax.dot_general(a, b, dims, preferred_element_type=F32)


def iota(shape, axis):
    return lax.broadcasted_iota(jnp.int32, shape, axis)


def swap_halves(x):
    return pltpu.roll(x, HALF, 1)


def split_halves(real, imag):
    first = iota(real.shape, 1) < HALF
    return (
        jnp.where(first, real, swap_halves(imag)),
        jnp.where(first, swap_halves(real), imag),
    )


def triangles(rows):
    upper = jnp.where(iota((BW, BW), 0) <= iota((BW, BW), 1), 1.0, 0.0).astype(BF16)
    lower = jnp.where(iota((rows, rows), 1) < iota((rows, rows), 0), 1.0, 0.0).astype(BF16)
    return upper, jnp.ones((BW, BW), BF16), lower


def position(ny):
    me = lax.axis_index("img")
    return me, lax.shift_right_logical(me, ny.bit_length()), lax.shift_right_logical(me, 1) & (ny - 1), me & 1


def target_kernel(devices, ny, nz, cap, owner, target):
    _, z, y, core = position(ny)
    own = owner[...]
    upper, ones, lower = triangles(own.shape[0])

    def rank(d, pos):
        member = jnp.where(own == d, 1.0, 0.0)
        bits = member.astype(BF16)
        before = dot(lower, dot(bits, ones).astype(BF16))
        return pos + member * (dot(bits, upper) - 1.0 + before)

    pos = jnp.zeros(own.shape, F32)
    if devices <= 16:
        for d in range(devices):
            pos = rank(d, pos)
    else:
        pos = lax.fori_loop(0, devices, rank, pos)
    rel_core = (own & 1) ^ core
    rel_y = (lax.shift_right_logical(own, 1) - y) & (ny - 1)
    rel_z = (lax.shift_right_logical(own, ny.bit_length()) - z) & (nz - 1)
    place = ((rel_z * ny + rel_y) * 2 + rel_core) * cap + pos.astype(jnp.int32)
    ref = 2 * iota(own.shape, 0) + jnp.where(iota(own.shape, 1) < KB, 0, 1)
    place = place + 8 - (ref & 7)
    target[...] = place + pltpu.roll(place, KB, 1) * 65536


def slice_kernel(*refs):
    sources, (slots, keep, send), held, arrived = refs[:5], refs[5:8], refs[8:13], refs[13]
    copies = [
        pltpu.make_async_copy(source, place, arrived.at[i])
        for i, (source, place) in enumerate(zip(sources, held))
    ]
    for copy in copies:
        copy.start()
    owner, local, table, volume, interp = held
    me = lax.axis_index("img")
    core = me & 1
    cap = keep.shape[0]
    for copy in copies[:3]:
        copy.wait()
    own = owner[...]
    rows = own.shape[0]
    upper, ones, lower = triangles(rows)
    member = own == me
    bits = jnp.where(member, 1.0, 0.0).astype(BF16)
    total = dot(bits, ones)
    before = dot(lower, total.astype(BF16))
    pos = (dot(bits, upper) - 1.0 + before).astype(jnp.int32)
    number = iota((rows, cap), 1).astype(F32)
    start, stop = before[:, 0:1], before[:, 0:1] + total[:, 0:1]
    row_hot = jnp.where(number >= start, jnp.where(number < stop, 1.0, 0.0), 0.0)
    loc = local[...]
    fields = [
        jnp.where(member, lax.shift_right_logical(pos, 7), 255),
        pos & 127,
        lax.shift_right_logical(loc, 8),
        loc & 255,
        table[...],
    ]
    fields = jnp.concatenate([f.astype(F32) for f in fields], axis=1).astype(BF16)
    found = dot(row_hot.T.astype(BF16), fields)
    slot = iota((cap, BW), 0).astype(F32)
    valid = slot < stop[rows - 1 : rows]
    hit = found[:, :BW] * 128.0 + found[:, BW : 2 * BW] == jnp.where(valid, slot, -1.0)
    place = jnp.where(hit, found[:, 2 * BW : 3 * BW] * 256.0 + found[:, 3 * BW : 4 * BW], 0.0)
    place = jnp.sum(place, axis=1, keepdims=True)
    place = jnp.where(valid[:, 0:1], place, -1.0)
    which = jnp.sum(jnp.where(hit, found[:, 4 * BW :], 0.0), axis=1, keepdims=True)
    column = iota((cap, 8), 1)
    slots[...] = jnp.where(column == 0, place, jnp.where(column == 1, which, 0.0))

    for copy in copies[3:]:
        copy.wait()
    depth = volume.shape[0]
    pick = jnp.where(iota((cap, depth), 1) == place.astype(jnp.int32), 1.0, 0.0).astype(BF16)
    voxels = dot(pick, volume[...])
    voxels = jnp.concatenate([voxels[:, :BW], voxels[:, BW:]], axis=0)
    which = jnp.concatenate([which, which], axis=0)
    tables = range(interp.shape[0])
    chosen = [jnp.where(which == float(t), voxels, 0.0).astype(BF16) for t in tables]
    matrix = jnp.concatenate([interp[t] for t in tables], axis=1)
    out = dot(jnp.concatenate(chosen, axis=1), matrix, NT)
    left, right = split_halves(out[:cap], out[cap:])
    keep[...] = jnp.where(core == 0, left, right).astype(BF16)
    send[...] = jnp.where(core == 0, right, left).astype(BF16)


def weigh_kernel(images, group, ctf, keep, send, squares):
    core = lax.axis_index("img") & 1
    count = images.shape[0]
    groups = ctf.shape[0]
    number = jnp.broadcast_to(group[...], (count, BW))

    def body(b, carry):
        lanes = pl.ds(pl.multiple_of(b * BW, BW), BW)
        scale = ctf[:, lanes]
        factor = jnp.zeros((count, BW), F32)
        for g in range(groups):
            factor = jnp.where(number == g, scale[g : g + 1], factor)
        real = images[:, pl.ds(pl.multiple_of(b * 2 * BW, BW), BW)].astype(F32) * factor
        imag = images[:, pl.ds(pl.multiple_of(b * 2 * BW + BW, BW), BW)].astype(F32) * factor
        left, right = split_halves(real, imag)
        keep[:, lanes] = jnp.where(core == 0, left, right).astype(BF16)
        send[:, lanes] = jnp.where(core == 0, right, left).astype(BF16)
        square = scale * scale
        left, right = split_halves(square, square)
        square = jnp.where(core == 0, left, right)
        high = square.astype(BF16)
        rest = square - high.astype(F32)
        squares[:, lanes] = jnp.concatenate([high.astype(F32), rest], axis=0).astype(BF16)
        return carry

    lax.fori_loop(0, KB, body, 0, unroll=8)


def rows_of(target, r, b):
    both = target[(r // 2) * BW + b]
    return both & 65535, lax.shift_right_logical(both, 16)


def score_kernel(
    places, target, group, cosine, sine, keep, other, squares, *rest
):
    pieces = rest[: len(places)]
    scores, gathered, norms, *stages = rest[len(places) :]
    blocks, lefts, powers = stages[0:2], stages[2:4], stages[4:6]
    shifts = cosine.shape[1]
    steps = KB // GROUP
    wide = GROUP * BW
    for piece, moves in zip(pieces, places):
        for source, size, start in moves:
            gathered[start + 8 : start + 8 + size, :] = piece[source : source + size, :].astype(F32)
    scores[...] = jnp.zeros(scores.shape, F32)
    norms[...] = jnp.zeros(norms.shape, F32)

    sublane = iota((8, BW), 0)

    def fetch(b, first):
        value = None
        for r in range(first, first + 8, 2):
            for i, row in enumerate(rows_of(target, r, b)):
                loaded = gathered[pl.ds(row, 8), :]
                value = loaded if value is None else jnp.where(sublane == r + i - first, loaded, value)
        return value

    def gather(step, block):
        for part in range(GROUP):
            for first in range(0, R, 8):
                block[part, first : first + 8, :] = fetch(step * GROUP + part, first)

    def rotate(step, block, left, power):
        for part in range(GROUP):
            b = step * GROUP + part
            lanes = slice(part * BW, (part + 1) * BW)
            value = block[part]
            swapped = swap_halves(value)
            for s in range(shifts):
                turned = value * cosine[b, s : s + 1, :] + swapped * sine[b, s : s + 1, :]
                left[s * R : (s + 1) * R, lanes] = turned.astype(BF16)
            square = value * value
            high = square.astype(BF16)
            power[0:R, lanes] = high
            power[R : 2 * R, lanes] = (square - high.astype(F32)).astype(BF16)

    def multiply(step, left, power):
        lanes = pl.ds(pl.multiple_of(step * wide, wide), wide)
        right = jnp.concatenate([keep[:, lanes], other[:, lanes]], axis=0)
        scores[...] += dot(left[...], right, NT)
        norms[...] += dot(power[...], squares[:, lanes], NT)

    def body(pair, carry):
        for half in range(2):
            step = 2 * pair + half
            gather(jnp.minimum(step + 1, steps - 1), blocks[1 - half])
            rotate(step, blocks[half], lefts[half], powers[half])
            multiply(jnp.maximum(step - 1, 0), lefts[1 - half], powers[1 - half])
        return carry

    gather(0, blocks[0])
    lefts[1][...] = jnp.zeros(lefts[1].shape, BF16)
    powers[1][...] = jnp.zeros(powers[1].shape, BF16)
    lax.fori_loop(0, steps // 2, body, 0)
    multiply(steps - 1, lefts[1], powers[1])
    half = squares.shape[0] // 2
    total = norms[...]
    total = total[:R, :half] + total[:R, half:] + total[R:, :half] + total[R:, half:]
    norm = jnp.zeros((R, scores.shape[1]), F32)
    for g in range(half):
        norm = jnp.where(group[...] == g, total[:, g : g + 1], norm)
    for s in range(shifts):
        scores[s * R : (s + 1) * R, :] -= 0.5 * norm


def back_kernel(ny, rows, order, target, mine, theirs, cosine, sine, keep, other, *rest):
    evidence = rest[0]
    placed = rest[-1]
    shifts = cosine.shape[1]
    scale = 1.0 / math.sqrt(KB * BW)
    placed[...] = jnp.zeros(placed.shape, F32)
    scores = (mine[...] + swap_halves(theirs[...])) * scale
    top = jnp.max(scores, axis=0, keepdims=True)
    exponent = jnp.exp(scores - top)
    total = jnp.sum(exponent, axis=0, keepdims=True)
    evidence[...] = top + jnp.log(total)
    weights = (exponent / total).astype(BF16)
    sublane = iota((8, BW), 0)

    def body(pair, carry):
        lanes = pl.ds(pl.multiple_of(pair * 2 * BW, BW), 2 * BW)
        right = jnp.concatenate([keep[:, lanes], other[:, lanes]], axis=0)
        sums = dot(weights, right)
        for part in range(2):
            b = pair * 2 + part
            straight = jnp.zeros((R, BW), F32)
            crossed = jnp.zeros((R, BW), F32)
            for s in range(shifts):
                term = sums[s * R : (s + 1) * R, part * BW : (part + 1) * BW]
                straight = straight + term * cosine[b, s : s + 1, :]
                crossed = crossed + term * sine[b, s : s + 1, :]
            value = straight + swap_halves(crossed)
            for r in range(0, R, 2):
                for i, row in enumerate(rows_of(target, r, b)):
                    k = (r + i) % 8
                    pltpu.store(
                        placed.at[pl.ds(row, 8), :],
                        value[r + i - k : r + i - k + 8],
                        mask=sublane == k,
                    )
        return carry

    lax.fori_loop(0, KB // 2, body, 0, unroll=4)
    for i, kz in enumerate(order):
        for ky in range(ny):
            start = (kz * ny + ky) * rows + 8
            rest[1 + i * ny + ky][...] = placed[start : start + rows, :].astype(BF16)


def adjoint_kernel(place, slots, volume, interp, keep, other, new_map):
    core = lax.axis_index("img") & 1
    cap = keep.shape[0]
    mine, theirs = keep[...], other[...]
    left = jnp.where(core == 0, mine, theirs)
    right = jnp.where(core == 0, theirs, mine)
    real, imag = split_halves(left, right)
    value = jnp.concatenate([real, imag], axis=0)
    which = slots[:, 1:2]
    which = jnp.concatenate([which, which], axis=0)
    tables = range(interp.shape[0])
    matrix = jnp.concatenate([interp[t] for t in tables], axis=0)
    high = value.astype(BF16).astype(F32)
    out = jnp.zeros((2 * cap, BW), F32)
    for part in (high, value - high):
        chosen = [jnp.where(which == float(t), part, 0.0).astype(BF16) for t in tables]
        out = out + dot(jnp.concatenate(chosen, axis=1), matrix)
    out = jnp.concatenate([out[:cap], out[cap:]], axis=1)
    depth = volume.shape[0]
    spread = jnp.where(
        iota((depth, cap), 0) == place[0:1, :].astype(jnp.int32), 1.0, 0.0
    ).astype(BF16)
    high = out.astype(BF16)
    rest = (out - high.astype(F32)).astype(BF16)
    new_map[...] = volume[...].astype(F32) + dot(
        jnp.concatenate([spread, spread], axis=1), jnp.concatenate([high, rest], axis=0)
    )


SMEM = pl.BlockSpec(memory_space=pltpu.SMEM)
VMEM = pl.BlockSpec(memory_space=pltpu.VMEM)
ANY = pl.BlockSpec(memory_space=pl.ANY)


def call(kernel, in_specs, out_shapes, scratch, flops, touched, name, limit=40):
    return pl.pallas_call(
        kernel,
        in_specs=in_specs,
        out_specs=[VMEM] * len(out_shapes),
        out_shape=out_shapes,
        scratch_shapes=scratch,
        compiler_params=pltpu.CompilerParams(vmem_limit_bytes=limit * 1024 * 1024),
        cost_estimate=pl.CostEstimate(flops=flops, bytes_accessed=touched, transcendentals=0),
        name=name,
    )


def per_device(images, groups, shifts, volume, owner, local, table_id, interp, ctf):
    devices = lax.axis_size("img")
    chips = devices // 2
    ny = 1 << ((chips.bit_length() - 1) // 2)
    nz = chips // ny
    me = lax.axis_index("img")
    core = me % 2
    cap = max(2, 3 * BLOCKS // (2 * devices))
    rows = 2 * cap
    count = images.shape[0]
    shift_count = shifts.shape[0]
    struct = jax.ShapeDtypeStruct

    def device(dz, dy, dc):
        return (dz * ny + dy) * 2 + dc

    everyone = [(dz, dy, dc) for dz in range(nz) for dy in range(ny) for dc in range(2)]
    core_pairs = [(device(*d), device(d[0], d[1], 1 - d[2])) for d in everyone]

    def along_z(k):
        return [(device(a, b, c), device((a + k) % nz, b, c)) for a, b, c in everyone]

    def along_y(k):
        return [(device(a, b, c), device(a, (b + k) % ny, c)) for a, b, c in everyone]

    def to(array, pairs):
        return lax.ppermute(array, "img", pairs)

    wide = (BLOCKS // BW, BW)
    owner = owner.reshape(wide)
    slots, slice_keep, slice_send = call(
        slice_kernel,
        [ANY] * 5,
        [struct((cap, 8), F32), struct((cap, BW), BF16), struct((cap, BW), BF16)],
        [pltpu.VMEM(wide, jnp.int32)] * 3
        + [
            pltpu.VMEM(volume.shape, BF16),
            pltpu.VMEM(interp.shape, BF16),
            pltpu.SemaphoreType.DMA((5,)),
        ],
        10**9,
        10**6,
        "own_slices",
        60,
    )(owner, local.reshape(wide), table_id.reshape(wide), volume, interp)
    own_piece = jnp.concatenate([slice_keep, to(slice_send, core_pairs)], axis=0)
    images, groups, _ = lax.optimization_barrier((images, groups, own_piece))

    near = sorted(range(1, nz), key=lambda k: min(k, nz - k))
    pieces = [(own_piece, [(0, rows, 0)])]
    by_z = {kz: to(own_piece, along_z(-kz)) for kz in near}
    for ky in range(1, ny):
        pieces.append((to(own_piece, along_y(-ky)), [(0, rows, ky * rows)]))
    for kz in near:
        start = kz * ny * rows
        pieces.append((by_z[kz], [(0, rows, start)]))
        for ky in range(1, ny):
            piece = to(by_z[kz], along_y(-ky))
            pieces.append((piece, [(0, rows, start + ky * rows)]))

    owner, shifts, _ = lax.optimization_barrier((owner, shifts, by_z[near[0]]))
    (target,) = call(
        functools.partial(target_kernel, devices, ny, nz, cap),
        [VMEM],
        [struct(wide, jnp.int32)],
        [],
        10**9,
        10**6,
        "target",
    )(owner)
    target = target.reshape(BLOCKS)

    weight_keep, weight_send, squares = call(
        weigh_kernel,
        [VMEM] * 3,
        [
            struct((count, KB * BW), BF16),
            struct((count, KB * BW), BF16),
            struct((2 * ctf.shape[0], KB * BW), BF16),
        ],
        [],
        10**9,
        4 * 10**6,
        "weigh",
    )(images, groups.reshape(count, 1), ctf)
    weight_other = to(weight_send, core_pairs)
    group_row = groups.astype(F32).reshape(1, count)
    group_row = jnp.concatenate([group_row, to(group_row, core_pairs)], axis=1).astype(jnp.int32)
    place = slots.T

    lane = jnp.arange(BW)
    freq_x = (lane % HALF + core * HALF - BW // 2).astype(F32)
    freq_y = jnp.arange(KB).astype(F32)
    shift_x = shifts[:, 0].astype(F32)
    shift_y = shifts[:, 1].astype(F32)
    angles = (
        2.0
        * math.pi
        / BW
        * (
            shift_x[None, :, None] * freq_x[None, None, :]
            + shift_y[None, :, None] * freq_y[:, None, None]
        )
    )
    cosine = jnp.cos(angles)
    sine = jnp.sin(angles) * jnp.where(lane < HALF, -1.0, 1.0)

    (partial,) = call(
        functools.partial(score_kernel, [moves for _, moves in pieces]),
        [SMEM] + [VMEM] * (6 + len(pieces)),
        [struct((shift_count * R, 2 * count), F32)],
        [
            pltpu.VMEM((chips * rows + 16, BW), F32),
            pltpu.VMEM((2 * R, 2 * ctf.shape[0]), F32),
        ]
        + [pltpu.VMEM((GROUP, R, BW), F32)] * 2
        + [pltpu.VMEM((shift_count * R, GROUP * BW), BF16)] * 2
        + [pltpu.VMEM((2 * R, GROUP * BW), BF16)] * 2,
        4 * 10**9,
        10**7,
        "score",
    )(target, group_row, cosine, sine, weight_keep, weight_other, squares, *[piece for piece, _ in pieces])

    theirs = to(partial, core_pairs)
    order = near[::-1] + [0]
    outs = call(
        functools.partial(back_kernel, ny, rows, order),
        [SMEM] + [VMEM] * 6,
        [struct((1, 2 * count), F32)]
        + [struct((rows, BW), BF16)] * chips,
        [pltpu.VMEM((chips * rows + 16, BW), F32)],
        4 * 10**9,
        10**7,
        "back",
    )(target, partial, theirs, cosine, sine, weight_keep, weight_other)
    evidence = outs[0][0, :count]
    parts = {kz: outs[1 + ny * i : 1 + ny * (i + 1)] for i, kz in enumerate(order)}
    moved = {kz: [to(parts[kz][ky], along_y(ky)) for ky in range(1, ny)] for kz in order}
    summed = {}
    for kz in order:
        summed[kz] = parts[kz][0].astype(F32)
        for part in moved[kz]:
            summed[kz] = summed[kz] + part.astype(F32)
    final = summed[0]
    for kz in near[::-1]:
        final = final + to(summed[kz].astype(BF16), along_z(kz)).astype(F32)
    sum_keep = final[:cap]
    sum_other = to(final[cap:], core_pairs)

    (new_map,) = call(
        adjoint_kernel,
        [VMEM] * 6,
        [struct(volume.shape, F32)],
        [],
        10**9,
        2 * 10**6,
        "adjoint",
    )(place, slots, volume, interp, sum_keep, sum_other)
    return (new_map, evidence)


def solution(mesh):
    return jax.shard_map(
        per_device,
        mesh=mesh,
        in_specs=(
            P(("parts", "img"), None),
            P(("parts", "img")),
            P("parts", None),
            P(("parts", "img"), None),
            P("parts", None),
            P("parts"),
            P("parts"),
            P(),
            P("parts", None),
        ),
        out_specs=(P(("parts", "img"), None), P(("parts", "img"))),
        check_vma=False,
    )
```

```python
import functools
import math

import jax
import jax.numpy as jnp
from jax import lax
from jax.experimental import pallas as pl
from jax.experimental.pallas import tpu as pltpu
from jax.sharding import PartitionSpec as P

BW = 128
KB = 64
R = 64
HALF = BW // 2
BLOCKS = R * KB
GROUP = 4

F32 = jnp.float32
BF16 = jnp.bfloat16
NT = (((1,), (1,)), ((), ()))
NN = (((1,), (0,)), ((), ()))


def dot(a, b, dims=NN):
    return lax.dot_general(a, b, dims, preferred_element_type=F32)


def iota(shape, axis):
    return lax.broadcasted_iota(jnp.int32, shape, axis)


def swap_halves(x):
    return pltpu.roll(x, HALF, 1)


def split_halves(real, imag):
    first = iota(real.shape, 1) < HALF
    return (
        jnp.where(first, real, swap_halves(imag)),
        jnp.where(first, swap_halves(real), imag),
    )


def triangles(rows):
    upper = jnp.where(iota((BW, BW), 0) <= iota((BW, BW), 1), 1.0, 0.0).astype(BF16)
    lower = jnp.where(iota((rows, rows), 1) < iota((rows, rows), 0), 1.0, 0.0).astype(BF16)
    return upper, jnp.ones((BW, BW), BF16), lower


def position(ny):
    me = lax.axis_index("img")
    return me, lax.shift_right_logical(me, ny.bit_length()), lax.shift_right_logical(me, 1) & (ny - 1), me & 1


def target_kernel(devices, ny, nz, cap, owner, target):
    _, z, y, core = position(ny)
    own = owner[...]
    upper, ones, lower = triangles(own.shape[0])

    def rank(d, pos):
        member = jnp.where(own == d, 1.0, 0.0)
        bits = member.astype(BF16)
        before = dot(lower, dot(bits, ones).astype(BF16))
        return pos + member * (dot(bits, upper) - 1.0 + before)

    pos = jnp.zeros(own.shape, F32)
    if devices <= 16:
        for d in range(devices):
            pos = rank(d, pos)
    else:
        pos = lax.fori_loop(0, devices, rank, pos)
    rel_core = (own & 1) ^ core
    rel_y = (lax.shift_right_logical(own, 1) - y) & (ny - 1)
    rel_z = (lax.shift_right_logical(own, ny.bit_length()) - z) & (nz - 1)
    place = ((rel_z * ny + rel_y) * 2 + rel_core) * cap + pos.astype(jnp.int32)
    ref = 2 * iota(own.shape, 0) + jnp.where(iota(own.shape, 1) < KB, 0, 1)
    place = place + 8 - (ref & 7)
    target[...] = place + pltpu.roll(place, KB, 1) * 65536


def slice_kernel(*refs):
    sources, (slots, keep, send), held, arrived = refs[:5], refs[5:8], refs[8:13], refs[13]
    copies = [
        pltpu.make_async_copy(source, place, arrived.at[i])
        for i, (source, place) in enumerate(zip(sources, held))
    ]
    for copy in copies:
        copy.start()
    owner, local, table, volume, interp = held
    me = lax.axis_index("img")
    core = me & 1
    cap = keep.shape[0]
    for copy in copies[:3]:
        copy.wait()
    own = owner[...]
    rows = own.shape[0]
    upper, ones, lower = triangles(rows)
    member = own == me
    bits = jnp.where(member, 1.0, 0.0).astype(BF16)
    total = dot(bits, ones)
    before = dot(lower, total.astype(BF16))
    pos = (dot(bits, upper) - 1.0 + before).astype(jnp.int32)
    number = iota((rows, cap), 1).astype(F32)
    start, stop = before[:, 0:1], before[:, 0:1] + total[:, 0:1]
    row_hot = jnp.where(number >= start, jnp.where(number < stop, 1.0, 0.0), 0.0)
    loc = local[...]
    fields = [
        jnp.where(member, lax.shift_right_logical(pos, 7), 255),
        pos & 127,
        lax.shift_right_logical(loc, 8),
        loc & 255,
        table[...],
    ]
    fields = jnp.concatenate([f.astype(F32) for f in fields], axis=1).astype(BF16)
    found = dot(row_hot.T.astype(BF16), fields)
    slot = iota((cap, BW), 0).astype(F32)
    valid = slot < stop[rows - 1 : rows]
    hit = found[:, :BW] * 128.0 + found[:, BW : 2 * BW] == jnp.where(valid, slot, -1.0)
    place = jnp.where(hit, found[:, 2 * BW : 3 * BW] * 256.0 + found[:, 3 * BW : 4 * BW], 0.0)
    place = jnp.sum(place, axis=1, keepdims=True)
    place = jnp.where(valid[:, 0:1], place, -1.0)
    which = jnp.sum(jnp.where(hit, found[:, 4 * BW :], 0.0), axis=1, keepdims=True)
    column = iota((cap, 8), 1)
    slots[...] = jnp.where(column == 0, place, jnp.where(column == 1, which, 0.0))

    for copy in copies[3:]:
        copy.wait()
    depth = volume.shape[0]
    pick = jnp.where(iota((cap, depth), 1) == place.astype(jnp.int32), 1.0, 0.0).astype(BF16)
    voxels = dot(pick, volume[...])
    voxels = jnp.concatenate([voxels[:, :BW], voxels[:, BW:]], axis=0)
    which = jnp.concatenate([which, which], axis=0)
    tables = range(interp.shape[0])
    chosen = [jnp.where(which == float(t), voxels, 0.0).astype(BF16) for t in tables]
    matrix = jnp.concatenate([interp[t] for t in tables], axis=1)
    out = dot(jnp.concatenate(chosen, axis=1), matrix, NT)
    left, right = split_halves(out[:cap], out[cap:])
    keep[...] = jnp.where(core == 0, left, right).astype(BF16)
    send[...] = jnp.where(core == 0, right, left).astype(BF16)


def weigh_kernel(images, group, ctf, keep, send, squares):
    core = lax.axis_index("img") & 1
    count = images.shape[0]
    groups = ctf.shape[0]
    number = jnp.broadcast_to(group[...], (count, BW))

    def body(b, carry):
        lanes = pl.ds(pl.multiple_of(b * BW, BW), BW)
        scale = ctf[:, lanes]
        factor = jnp.zeros((count, BW), F32)
        for g in range(groups):
            factor = jnp.where(number == g, scale[g : g + 1], factor)
        real = images[:, pl.ds(pl.multiple_of(b * 2 * BW, BW), BW)].astype(F32) * factor
        imag = images[:, pl.ds(pl.multiple_of(b * 2 * BW + BW, BW), BW)].astype(F32) * factor
        left, right = split_halves(real, imag)
        keep[:, lanes] = jnp.where(core == 0, left, right).astype(BF16)
        send[:, lanes] = jnp.where(core == 0, right, left).astype(BF16)
        square = scale * scale
        left, right = split_halves(square, square)
        square = jnp.where(core == 0, left, right)
        high = square.astype(BF16)
        rest = square - high.astype(F32)
        squares[:, lanes] = jnp.concatenate([high.astype(F32), rest], axis=0).astype(BF16)
        return carry

    lax.fori_loop(0, KB, body, 0, unroll=8)


def rows_of(target, r, b):
    both = target[(r // 2) * BW + b]
    return both & 65535, lax.shift_right_logical(both, 16)


def score_kernel(
    places, target, group, cosine, sine, keep, other, squares, *rest
):
    pieces = rest[: len(places)]
    scores, gathered, norms, *stages = rest[len(places) :]
    blocks, lefts, powers = stages[0:2], stages[2:4], stages[4:6]
    shifts = cosine.shape[1]
    steps = KB // GROUP
    wide = GROUP * BW
    for piece, moves in zip(pieces, places):
        for source, size, start in moves:
            gathered[start + 8 : start + 8 + size, :] = piece[source : source + size, :].astype(F32)
    scores[...] = jnp.zeros(scores.shape, F32)
    norms[...] = jnp.zeros(norms.shape, F32)

    sublane = iota((8, BW), 0)

    def fetch(b, first):
        value = None
        for r in range(first, first + 8, 2):
            for i, row in enumerate(rows_of(target, r, b)):
                loaded = gathered[pl.ds(row, 8), :]
                value = loaded if value is None else jnp.where(sublane == r + i - first, loaded, value)
        return value

    def gather(step, block):
        for part in range(GROUP):
            for first in range(0, R, 8):
                block[part, first : first + 8, :] = fetch(step * GROUP + part, first)

    def rotate(step, block, left, power):
        for part in range(GROUP):
            b = step * GROUP + part
            lanes = slice(part * BW, (part + 1) * BW)
            value = block[part]
            swapped = swap_halves(value)
            for s in range(shifts):
                turned = value * cosine[b, s : s + 1, :] + swapped * sine[b, s : s + 1, :]
                left[s * R : (s + 1) * R, lanes] = turned.astype(BF16)
            square = value * value
            high = square.astype(BF16)
            power[0:R, lanes] = high
            power[R : 2 * R, lanes] = (square - high.astype(F32)).astype(BF16)

    def multiply(step, left, power):
        lanes = pl.ds(pl.multiple_of(step * wide, wide), wide)
        right = jnp.concatenate([keep[:, lanes], other[:, lanes]], axis=0)
        scores[...] += dot(left[...], right, NT)
        norms[...] += dot(power[...], squares[:, lanes], NT)

    def body(pair, carry):
        for half in range(2):
            step = 2 * pair + half
            gather(jnp.minimum(step + 1, steps - 1), blocks[1 - half])
            rotate(step, blocks[half], lefts[half], powers[half])
            multiply(jnp.maximum(step - 1, 0), lefts[1 - half], powers[1 - half])
        return carry

    gather(0, blocks[0])
    lefts[1][...] = jnp.zeros(lefts[1].shape, BF16)
    powers[1][...] = jnp.zeros(powers[1].shape, BF16)
    lax.fori_loop(0, steps // 2, body, 0)
    multiply(steps - 1, lefts[1], powers[1])
    half = squares.shape[0] // 2
    total = norms[...]
    total = total[:R, :half] + total[:R, half:] + total[R:, :half] + total[R:, half:]
    norm = jnp.zeros((R, scores.shape[1]), F32)
    for g in range(half):
        norm = jnp.where(group[...] == g, total[:, g : g + 1], norm)
    for s in range(shifts):
        scores[s * R : (s + 1) * R, :] -= 0.5 * norm


def back_kernel(ny, rows, order, target, mine, theirs, cosine, sine, keep, other, *rest):
    evidence = rest[0]
    placed = rest[-1]
    shifts = cosine.shape[1]
    scale = 1.0 / math.sqrt(KB * BW)
    placed[...] = jnp.zeros(placed.shape, F32)
    scores = (mine[...] + swap_halves(theirs[...])) * scale
    top = jnp.max(scores, axis=0, keepdims=True)
    exponent = jnp.exp(scores - top)
    total = jnp.sum(exponent, axis=0, keepdims=True)
    evidence[...] = top + jnp.log(total)
    weights = (exponent / total).astype(BF16)
    sublane = iota((8, BW), 0)

    def body(pair, carry):
        lanes = pl.ds(pl.multiple_of(pair * 2 * BW, BW), 2 * BW)
        right = jnp.concatenate([keep[:, lanes], other[:, lanes]], axis=0)
        sums = dot(weights, right)
        for part in range(2):
            b = pair * 2 + part
            straight = jnp.zeros((R, BW), F32)
            crossed = jnp.zeros((R, BW), F32)
            for s in range(shifts):
                term = sums[s * R : (s + 1) * R, part * BW : (part + 1) * BW]
                straight = straight + term * cosine[b, s : s + 1, :]
                crossed = crossed + term * sine[b, s : s + 1, :]
            value = straight + swap_halves(crossed)
            for r in range(0, R, 2):
                for i, row in enumerate(rows_of(target, r, b)):
                    k = (r + i) % 8
                    pltpu.store(
                        placed.at[pl.ds(row, 8), :],
                        value[r + i - k : r + i - k + 8],
                        mask=sublane == k,
                    )
        return carry

    lax.fori_loop(0, KB // 2, body, 0, unroll=4)
    for i, kz in enumerate(order):
        for ky in range(ny):
            start = (kz * ny + ky) * rows + 8
            rest[1 + i * ny + ky][...] = placed[start : start + rows, :].astype(BF16)


def interpolate_back(value, slots, interp, core):
    which = jnp.broadcast_to(slots[:, 1:2], value.shape)
    tables = range(interp.shape[0])
    blank = jnp.zeros((HALF, BW), BF16)
    matrix = []
    for t in tables:
        half = jnp.where(core == 0, interp[t][:HALF], interp[t][HALF:])
        matrix += [jnp.concatenate(pair, axis=1) for pair in ((half, blank), (blank, half))]
    matrix = jnp.concatenate(matrix, axis=0)
    high = value.astype(BF16).astype(F32)
    out = jnp.zeros((value.shape[0], 2 * BW), F32)
    for part in (high, value - high):
        chosen = [jnp.where(which == float(t), part, 0.0).astype(BF16) for t in tables]
        out = out + dot(jnp.concatenate(chosen, axis=1), matrix)
    return out


def own_half_kernel(place, slots, interp, keep, half, spread):
    core = lax.axis_index("img") & 1
    half[...] = interpolate_back(keep[...], slots, interp, core)
    spread[...] = jnp.where(
        iota(spread.shape, 0) == place[0:1, :].astype(jnp.int32), 1.0, 0.0
    ).astype(BF16)


def adjoint_kernel(slots, volume, interp, half, spread, other, new_map):
    core = lax.axis_index("img") & 1
    out = half[...] + interpolate_back(other[...], slots, interp, 1 - core)
    high = out.astype(BF16)
    rest = (out - high.astype(F32)).astype(BF16)
    hot = spread[...]
    new_map[...] = volume[...].astype(F32) + dot(
        jnp.concatenate([hot, hot], axis=1), jnp.concatenate([high, rest], axis=0)
    )


SMEM = pl.BlockSpec(memory_space=pltpu.SMEM)
VMEM = pl.BlockSpec(memory_space=pltpu.VMEM)
ANY = pl.BlockSpec(memory_space=pl.ANY)


def call(kernel, in_specs, out_shapes, scratch, flops, touched, name, limit=40):
    return pl.pallas_call(
        kernel,
        in_specs=in_specs,
        out_specs=[VMEM] * len(out_shapes),
        out_shape=out_shapes,
        scratch_shapes=scratch,
        compiler_params=pltpu.CompilerParams(vmem_limit_bytes=limit * 1024 * 1024),
        cost_estimate=pl.CostEstimate(flops=flops, bytes_accessed=touched, transcendentals=0),
        name=name,
    )


def per_device(images, groups, shifts, volume, owner, local, table_id, interp, ctf):
    devices = lax.axis_size("img")
    chips = devices // 2
    ny = 1 << ((chips.bit_length() - 1) // 2)
    nz = chips // ny
    me = lax.axis_index("img")
    core = me % 2
    cap = max(2, 3 * BLOCKS // (2 * devices))
    rows = 2 * cap
    count = images.shape[0]
    shift_count = shifts.shape[0]
    struct = jax.ShapeDtypeStruct

    def device(dz, dy, dc):
        return (dz * ny + dy) * 2 + dc

    everyone = [(dz, dy, dc) for dz in range(nz) for dy in range(ny) for dc in range(2)]
    core_pairs = [(device(*d), device(d[0], d[1], 1 - d[2])) for d in everyone]

    def along_z(k):
        return [(device(a, b, c), device((a + k) % nz, b, c)) for a, b, c in everyone]

    def along_y(k):
        return [(device(a, b, c), device(a, (b + k) % ny, c)) for a, b, c in everyone]

    def to(array, pairs):
        return lax.ppermute(array, "img", pairs)

    wide = (BLOCKS // BW, BW)
    owner = owner.reshape(wide)
    slots, slice_keep, slice_send = call(
        slice_kernel,
        [ANY] * 5,
        [struct((cap, 8), F32), struct((cap, BW), BF16), struct((cap, BW), BF16)],
        [pltpu.VMEM(wide, jnp.int32)] * 3
        + [
            pltpu.VMEM(volume.shape, BF16),
            pltpu.VMEM(interp.shape, BF16),
            pltpu.SemaphoreType.DMA((5,)),
        ],
        10**9,
        10**6,
        "own_slices",
        60,
    )(owner, local.reshape(wide), table_id.reshape(wide), volume, interp)
    own_piece = jnp.concatenate([slice_keep, to(slice_send, core_pairs)], axis=0)
    images, groups, _ = lax.optimization_barrier((images, groups, own_piece))

    near = sorted(range(1, nz), key=lambda k: min(k, nz - k))
    pieces = [(own_piece, [(0, rows, 0)])]
    by_z = {kz: to(own_piece, along_z(-kz)) for kz in near}
    for ky in range(1, ny):
        pieces.append((to(own_piece, along_y(-ky)), [(0, rows, ky * rows)]))
    for kz in near:
        start = kz * ny * rows
        pieces.append((by_z[kz], [(0, rows, start)]))
        for ky in range(1, ny):
            piece = to(by_z[kz], along_y(-ky))
            pieces.append((piece, [(0, rows, start + ky * rows)]))

    owner, shifts, _ = lax.optimization_barrier((owner, shifts, by_z[near[0]]))
    (target,) = call(
        functools.partial(target_kernel, devices, ny, nz, cap),
        [VMEM],
        [struct(wide, jnp.int32)],
        [],
        10**9,
        10**6,
        "target",
    )(owner)
    target = target.reshape(BLOCKS)

    weight_keep, weight_send, squares = call(
        weigh_kernel,
        [VMEM] * 3,
        [
            struct((count, KB * BW), BF16),
            struct((count, KB * BW), BF16),
            struct((2 * ctf.shape[0], KB * BW), BF16),
        ],
        [],
        10**9,
        4 * 10**6,
        "weigh",
    )(images, groups.reshape(count, 1), ctf)
    weight_other = to(weight_send, core_pairs)
    group_row = groups.astype(F32).reshape(1, count)
    group_row = jnp.concatenate([group_row, to(group_row, core_pairs)], axis=1).astype(jnp.int32)
    place = slots.T

    lane = jnp.arange(BW)
    freq_x = (lane % HALF + core * HALF - BW // 2).astype(F32)
    freq_y = jnp.arange(KB).astype(F32)
    shift_x = shifts[:, 0].astype(F32)
    shift_y = shifts[:, 1].astype(F32)
    angles = (
        2.0
        * math.pi
        / BW
        * (
            shift_x[None, :, None] * freq_x[None, None, :]
            + shift_y[None, :, None] * freq_y[:, None, None]
        )
    )
    cosine = jnp.cos(angles)
    sine = jnp.sin(angles) * jnp.where(lane < HALF, -1.0, 1.0)

    (partial,) = call(
        functools.partial(score_kernel, [moves for _, moves in pieces]),
        [SMEM] + [VMEM] * (6 + len(pieces)),
        [struct((shift_count * R, 2 * count), F32)],
        [
            pltpu.VMEM((chips * rows + 16, BW), F32),
            pltpu.VMEM((2 * R, 2 * ctf.shape[0]), F32),
        ]
        + [pltpu.VMEM((GROUP, R, BW), F32)] * 2
        + [pltpu.VMEM((shift_count * R, GROUP * BW), BF16)] * 2
        + [pltpu.VMEM((2 * R, GROUP * BW), BF16)] * 2,
        4 * 10**9,
        10**7,
        "score",
    )(target, group_row, cosine, sine, weight_keep, weight_other, squares, *[piece for piece, _ in pieces])

    theirs = to(partial, core_pairs)
    order = near[::-1] + [0]
    outs = call(
        functools.partial(back_kernel, ny, rows, order),
        [SMEM] + [VMEM] * 6,
        [struct((1, 2 * count), F32)]
        + [struct((rows, BW), BF16)] * chips,
        [pltpu.VMEM((chips * rows + 16, BW), F32)],
        4 * 10**9,
        10**7,
        "back",
    )(target, partial, theirs, cosine, sine, weight_keep, weight_other)
    evidence = outs[0][0, :count]
    parts = {kz: outs[1 + ny * i : 1 + ny * (i + 1)] for i, kz in enumerate(order)}
    moved = {kz: [to(parts[kz][ky], along_y(ky)) for ky in range(1, ny)] for kz in order}
    crossed = {}
    for kz in order:
        total = parts[kz][0].astype(F32)
        for part in moved[kz]:
            total = total + part.astype(F32)
        crossed[kz] = to(total.astype(BF16), along_z(kz)) if kz else total

    def total_of(span):
        total = crossed[0][span]
        for kz in near[::-1]:
            total = total + crossed[kz][span].astype(F32)
        return total

    sum_other = to(total_of(slice(cap, rows)), core_pairs)
    sum_keep = total_of(slice(0, cap))

    half, spread = call(
        own_half_kernel,
        [VMEM] * 4,
        [struct((cap, 2 * BW), F32), struct((volume.shape[0], cap), BF16)],
        [],
        10**9,
        2 * 10**6,
        "own_half",
    )(place, slots, interp, sum_keep)
    (new_map,) = call(
        adjoint_kernel,
        [VMEM] * 6,
        [struct(volume.shape, F32)],
        [],
        10**9,
        2 * 10**6,
        "adjoint",
    )(slots, volume, interp, half, spread, sum_other)
    return (new_map, evidence)


def solution(mesh):
    return jax.shard_map(
        per_device,
        mesh=mesh,
        in_specs=(
            P(("parts", "img"), None),
            P(("parts", "img")),
            P("parts", None),
            P(("parts", "img"), None),
            P("parts", None),
            P("parts"),
            P("parts"),
            P(),
            P("parts", None),
        ),
        out_specs=(P(("parts", "img"), None), P(("parts", "img"))),
        check_vma=False,
    )
```

```python
import functools
import math

import jax
import jax.numpy as jnp
from jax import lax
from jax.experimental import pallas as pl
from jax.experimental.pallas import tpu as pltpu
from jax.sharding import PartitionSpec as P

BW = 128
KB = 64
R = 64
HALF = BW // 2
BLOCKS = R * KB
GROUP = 4
PARTS = 4

F32 = jnp.float32
BF16 = jnp.bfloat16
NT = (((1,), (1,)), ((), ()))
NN = (((1,), (0,)), ((), ()))


def dot(a, b, dims=NN):
    return lax.dot_general(a, b, dims, preferred_element_type=F32)


def iota(shape, axis):
    return lax.broadcasted_iota(jnp.int32, shape, axis)


def swap_halves(x):
    return pltpu.roll(x, HALF, 1)


def split_halves(real, imag):
    first = iota(real.shape, 1) < HALF
    return (
        jnp.where(first, real, swap_halves(imag)),
        jnp.where(first, swap_halves(real), imag),
    )


def triangles(rows):
    upper = jnp.where(iota((BW, BW), 0) <= iota((BW, BW), 1), 1.0, 0.0).astype(BF16)
    lower = jnp.where(iota((rows, rows), 1) < iota((rows, rows), 0), 1.0, 0.0).astype(BF16)
    return upper, jnp.ones((BW, BW), BF16), lower


def position(ny):
    me = lax.axis_index("img")
    return me, lax.shift_right_logical(me, ny.bit_length()), lax.shift_right_logical(me, 1) & (ny - 1), me & 1


def target_kernel(devices, ny, nz, cap, owner, target):
    _, z, y, core = position(ny)
    own = owner[...]
    upper, ones, lower = triangles(own.shape[0])

    def rank(d, pos):
        member = jnp.where(own == d, 1.0, 0.0)
        bits = member.astype(BF16)
        before = dot(lower, dot(bits, ones).astype(BF16))
        return pos + member * (dot(bits, upper) - 1.0 + before)

    pos = jnp.zeros(own.shape, F32)
    if devices <= 16:
        for d in range(devices):
            pos = rank(d, pos)
    else:
        pos = lax.fori_loop(0, devices, rank, pos)
    rel_core = (own & 1) ^ core
    rel_y = (lax.shift_right_logical(own, 1) - y) & (ny - 1)
    rel_z = (lax.shift_right_logical(own, ny.bit_length()) - z) & (nz - 1)
    place = ((rel_z * ny + rel_y) * 2 + rel_core) * cap + pos.astype(jnp.int32)
    ref = 2 * iota(own.shape, 0) + jnp.where(iota(own.shape, 1) < KB, 0, 1)
    place = place + 8 - (ref & 7)
    target[...] = place + pltpu.roll(place, KB, 1) * 65536


def slice_kernel(*refs):
    sources, (slots, keep, send), held, arrived = refs[:5], refs[5:8], refs[8:13], refs[13]
    copies = [
        pltpu.make_async_copy(source, place, arrived.at[i])
        for i, (source, place) in enumerate(zip(sources, held))
    ]
    for copy in copies:
        copy.start()
    owner, local, table, volume, interp = held
    me = lax.axis_index("img")
    core = me & 1
    cap = keep.shape[0]
    for copy in copies[:3]:
        copy.wait()
    own = owner[...]
    rows = own.shape[0]
    upper, ones, lower = triangles(rows)
    member = own == me
    bits = jnp.where(member, 1.0, 0.0).astype(BF16)
    total = dot(bits, ones)
    before = dot(lower, total.astype(BF16))
    pos = (dot(bits, upper) - 1.0 + before).astype(jnp.int32)
    number = iota((rows, cap), 1).astype(F32)
    start, stop = before[:, 0:1], before[:, 0:1] + total[:, 0:1]
    row_hot = jnp.where(number >= start, jnp.where(number < stop, 1.0, 0.0), 0.0)
    loc = local[...]
    fields = [
        jnp.where(member, lax.shift_right_logical(pos, 7), 255),
        pos & 127,
        lax.shift_right_logical(loc, 8),
        loc & 255,
        table[...],
    ]
    fields = jnp.concatenate([f.astype(F32) for f in fields], axis=1).astype(BF16)
    found = dot(row_hot.T.astype(BF16), fields)
    slot = iota((cap, BW), 0).astype(F32)
    valid = slot < stop[rows - 1 : rows]
    hit = found[:, :BW] * 128.0 + found[:, BW : 2 * BW] == jnp.where(valid, slot, -1.0)
    place = jnp.where(hit, found[:, 2 * BW : 3 * BW] * 256.0 + found[:, 3 * BW : 4 * BW], 0.0)
    place = jnp.sum(place, axis=1, keepdims=True)
    place = jnp.where(valid[:, 0:1], place, -1.0)
    which = jnp.sum(jnp.where(hit, found[:, 4 * BW :], 0.0), axis=1, keepdims=True)
    column = iota((cap, 8), 1)
    slots[...] = jnp.where(column == 0, place, jnp.where(column == 1, which, 0.0))

    for copy in copies[3:]:
        copy.wait()
    depth = volume.shape[0]
    pick = jnp.where(iota((cap, depth), 1) == place.astype(jnp.int32), 1.0, 0.0).astype(BF16)
    voxels = dot(pick, volume[...])
    voxels = jnp.concatenate([voxels[:, :BW], voxels[:, BW:]], axis=0)
    which = jnp.concatenate([which, which], axis=0)
    tables = range(interp.shape[0])
    chosen = [jnp.where(which == float(t), voxels, 0.0).astype(BF16) for t in tables]
    matrix = jnp.concatenate([interp[t] for t in tables], axis=1)
    out = dot(jnp.concatenate(chosen, axis=1), matrix, NT)
    left, right = split_halves(out[:cap], out[cap:])
    keep[...] = jnp.where(core == 0, left, right).astype(BF16)
    send[...] = jnp.where(core == 0, right, left).astype(BF16)


def weigh_kernel(images, group, ctf, keep, send, squares):
    core = lax.axis_index("img") & 1
    count = images.shape[0]
    groups = ctf.shape[0]
    number = jnp.broadcast_to(group[...], (count, BW))

    def body(b, carry):
        lanes = pl.ds(pl.multiple_of(b * BW, BW), BW)
        scale = ctf[:, lanes]
        factor = jnp.zeros((count, BW), F32)
        for g in range(groups):
            factor = jnp.where(number == g, scale[g : g + 1], factor)
        real = images[:, pl.ds(pl.multiple_of(b * 2 * BW, BW), BW)].astype(F32) * factor
        imag = images[:, pl.ds(pl.multiple_of(b * 2 * BW + BW, BW), BW)].astype(F32) * factor
        left, right = split_halves(real, imag)
        keep[:, lanes] = jnp.where(core == 0, left, right).astype(BF16)
        send[:, lanes] = jnp.where(core == 0, right, left).astype(BF16)
        square = scale * scale
        left, right = split_halves(square, square)
        square = jnp.where(core == 0, left, right)
        high = square.astype(BF16)
        rest = square - high.astype(F32)
        squares[:, lanes] = jnp.concatenate([high.astype(F32), rest], axis=0).astype(BF16)
        return carry

    lax.fori_loop(0, KB, body, 0, unroll=8)


def rows_of(target, r, b):
    both = target[(r // 2) * BW + b]
    return both & 65535, lax.shift_right_logical(both, 16)


def score_kernel(
    places, target, group, cosine, sine, keep, other, squares, *rest
):
    pieces = rest[: len(places)]
    scores, gathered, norms, *stages = rest[len(places) :]
    blocks, lefts, powers = stages[0:2], stages[2:4], stages[4:6]
    shifts = cosine.shape[1]
    steps = KB // GROUP
    wide = GROUP * BW
    for piece, moves in zip(pieces, places):
        for source, size, start in moves:
            gathered[start + 8 : start + 8 + size, :] = piece[source : source + size, :].astype(F32)
    scores[...] = jnp.zeros(scores.shape, F32)
    norms[...] = jnp.zeros(norms.shape, F32)

    sublane = iota((8, BW), 0)

    def fetch(b, first):
        value = None
        for r in range(first, first + 8, 2):
            for i, row in enumerate(rows_of(target, r, b)):
                loaded = gathered[pl.ds(row, 8), :]
                value = loaded if value is None else jnp.where(sublane == r + i - first, loaded, value)
        return value

    def gather(step, block):
        for part in range(GROUP):
            for first in range(0, R, 8):
                block[part, first : first + 8, :] = fetch(step * GROUP + part, first)

    def rotate(step, block, left, power):
        for part in range(GROUP):
            b = step * GROUP + part
            lanes = slice(part * BW, (part + 1) * BW)
            value = block[part]
            swapped = swap_halves(value)
            for s in range(shifts):
                turned = value * cosine[b, s : s + 1, :] + swapped * sine[b, s : s + 1, :]
                left[s * R : (s + 1) * R, lanes] = turned.astype(BF16)
            square = value * value
            high = square.astype(BF16)
            power[0:R, lanes] = high
            power[R : 2 * R, lanes] = (square - high.astype(F32)).astype(BF16)

    def multiply(step, left, power):
        lanes = pl.ds(pl.multiple_of(step * wide, wide), wide)
        right = jnp.concatenate([keep[:, lanes], other[:, lanes]], axis=0)
        scores[...] += dot(left[...], right, NT)
        norms[...] += dot(power[...], squares[:, lanes], NT)

    def body(pair, carry):
        for half in range(2):
            step = 2 * pair + half
            gather(jnp.minimum(step + 1, steps - 1), blocks[1 - half])
            rotate(step, blocks[half], lefts[half], powers[half])
            multiply(jnp.maximum(step - 1, 0), lefts[1 - half], powers[1 - half])
        return carry

    gather(0, blocks[0])
    lefts[1][...] = jnp.zeros(lefts[1].shape, BF16)
    powers[1][...] = jnp.zeros(powers[1].shape, BF16)
    lax.fori_loop(0, steps // 2, body, 0)
    multiply(steps - 1, lefts[1], powers[1])
    half = squares.shape[0] // 2
    total = norms[...]
    total = total[:R, :half] + total[:R, half:] + total[R:, :half] + total[R:, half:]
    norm = jnp.zeros((R, scores.shape[1]), F32)
    for g in range(half):
        norm = jnp.where(group[...] == g, total[:, g : g + 1], norm)
    for s in range(shifts):
        scores[s * R : (s + 1) * R, :] -= 0.5 * norm


def back_kernel(ny, rows, order, target, mine, theirs, cosine, sine, keep, other, *rest):
    evidence = rest[0]
    placed = rest[-1]
    shifts = cosine.shape[1]
    scale = 1.0 / math.sqrt(KB * BW)
    placed[...] = jnp.zeros(placed.shape, F32)
    scores = (mine[...] + swap_halves(theirs[...])) * scale
    top = jnp.max(scores, axis=0, keepdims=True)
    exponent = jnp.exp(scores - top)
    total = jnp.sum(exponent, axis=0, keepdims=True)
    evidence[...] = top + jnp.log(total)
    weights = (exponent / total).astype(BF16)
    sublane = iota((8, BW), 0)

    def body(pair, carry):
        lanes = pl.ds(pl.multiple_of(pair * 2 * BW, BW), 2 * BW)
        right = jnp.concatenate([keep[:, lanes], other[:, lanes]], axis=0)
        sums = dot(weights, right)
        for part in range(2):
            b = pair * 2 + part
            straight = jnp.zeros((R, BW), F32)
            crossed = jnp.zeros((R, BW), F32)
            for s in range(shifts):
                term = sums[s * R : (s + 1) * R, part * BW : (part + 1) * BW]
                straight = straight + term * cosine[b, s : s + 1, :]
                crossed = crossed + term * sine[b, s : s + 1, :]
            value = straight + swap_halves(crossed)
            for r in range(0, R, 2):
                for i, row in enumerate(rows_of(target, r, b)):
                    k = (r + i) % 8
                    pltpu.store(
                        placed.at[pl.ds(row, 8), :],
                        value[r + i - k : r + i - k + 8],
                        mask=sublane == k,
                    )
        return carry

    lax.fori_loop(0, KB // 2, body, 0, unroll=4)
    for i, kz in enumerate(order):
        for ky in range(ny):
            start = (kz * ny + ky) * rows + 8
            rest[1 + i * ny + ky][...] = placed[start : start + rows, :].astype(BF16)


def interpolate_back(value, slots, interp, core):
    which = jnp.broadcast_to(slots[:, 1:2], value.shape)
    tables = range(interp.shape[0])
    blank = jnp.zeros((HALF, BW), BF16)
    matrix = []
    for t in tables:
        half = jnp.where(core == 0, interp[t][:HALF], interp[t][HALF:])
        matrix += [jnp.concatenate(pair, axis=1) for pair in ((half, blank), (blank, half))]
    matrix = jnp.concatenate(matrix, axis=0)
    high = value.astype(BF16).astype(F32)
    out = jnp.zeros((value.shape[0], 2 * BW), F32)
    for part in (high, value - high):
        chosen = [jnp.where(which == float(t), part, 0.0).astype(BF16) for t in tables]
        out = out + dot(jnp.concatenate(chosen, axis=1), matrix)
    return out


def own_half_kernel(place, slots, interp, keep, half, spread):
    core = lax.axis_index("img") & 1
    half[...] = interpolate_back(keep[...], slots, interp, core)
    spread[...] = jnp.where(
        iota(spread.shape, 0) == place[0:1, :].astype(jnp.int32), 1.0, 0.0
    ).astype(BF16)


def adjoint_kernel(slots, volume, interp, half, spread, other, new_map, held, sent):
    core = lax.axis_index("img") & 1
    out = half[...] + interpolate_back(other[...], slots, interp, 1 - core)
    high = out.astype(BF16)
    rest = (out - high.astype(F32)).astype(BF16)
    sums = jnp.concatenate([high, rest], axis=0)
    size = volume.shape[0] // PARTS
    copies = []
    for part in range(PARTS):
        rows = slice(part * size, (part + 1) * size)
        hot = spread[rows, :]
        held[rows, :] = volume[rows, :].astype(F32) + dot(
            jnp.concatenate([hot, hot], axis=1), sums
        )
        copy = pltpu.make_async_copy(held.at[rows, :], new_map.at[rows, :], sent.at[part])
        copy.start()
        copies.append(copy)
    for copy in copies:
        copy.wait()


SMEM = pl.BlockSpec(memory_space=pltpu.SMEM)
VMEM = pl.BlockSpec(memory_space=pltpu.VMEM)
ANY = pl.BlockSpec(memory_space=pl.ANY)


def call(kernel, in_specs, out_shapes, scratch, flops, touched, name, limit=40, out=VMEM):
    return pl.pallas_call(
        kernel,
        in_specs=in_specs,
        out_specs=[out] * len(out_shapes),
        out_shape=out_shapes,
        scratch_shapes=scratch,
        compiler_params=pltpu.CompilerParams(vmem_limit_bytes=limit * 1024 * 1024),
        cost_estimate=pl.CostEstimate(flops=flops, bytes_accessed=touched, transcendentals=0),
        name=name,
    )


def per_device(images, groups, shifts, volume, owner, local, table_id, interp, ctf):
    devices = lax.axis_size("img")
    chips = devices // 2
    ny = 1 << ((chips.bit_length() - 1) // 2)
    nz = chips // ny
    me = lax.axis_index("img")
    core = me % 2
    cap = max(2, 3 * BLOCKS // (2 * devices))
    rows = 2 * cap
    count = images.shape[0]
    shift_count = shifts.shape[0]
    struct = jax.ShapeDtypeStruct

    def device(dz, dy, dc):
        return (dz * ny + dy) * 2 + dc

    everyone = [(dz, dy, dc) for dz in range(nz) for dy in range(ny) for dc in range(2)]
    core_pairs = [(device(*d), device(d[0], d[1], 1 - d[2])) for d in everyone]

    def along_z(k):
        return [(device(a, b, c), device((a + k) % nz, b, c)) for a, b, c in everyone]

    def along_y(k):
        return [(device(a, b, c), device(a, (b + k) % ny, c)) for a, b, c in everyone]

    def to(array, pairs):
        return lax.ppermute(array, "img", pairs)

    wide = (BLOCKS // BW, BW)
    owner = owner.reshape(wide)
    slots, slice_keep, slice_send = call(
        slice_kernel,
        [ANY] * 5,
        [struct((cap, 8), F32), struct((cap, BW), BF16), struct((cap, BW), BF16)],
        [pltpu.VMEM(wide, jnp.int32)] * 3
        + [
            pltpu.VMEM(volume.shape, BF16),
            pltpu.VMEM(interp.shape, BF16),
            pltpu.SemaphoreType.DMA((5,)),
        ],
        10**9,
        10**6,
        "own_slices",
        60,
    )(owner, local.reshape(wide), table_id.reshape(wide), volume, interp)
    own_piece = jnp.concatenate([slice_keep, to(slice_send, core_pairs)], axis=0)
    images, groups, _ = lax.optimization_barrier((images, groups, own_piece))

    near = sorted(range(1, nz), key=lambda k: min(k, nz - k))
    pieces = [(own_piece, [(0, rows, 0)])]
    by_z = {kz: to(own_piece, along_z(-kz)) for kz in near}
    for ky in range(1, ny):
        pieces.append((to(own_piece, along_y(-ky)), [(0, rows, ky * rows)]))
    for kz in near:
        start = kz * ny * rows
        pieces.append((by_z[kz], [(0, rows, start)]))
        for ky in range(1, ny):
            piece = to(by_z[kz], along_y(-ky))
            pieces.append((piece, [(0, rows, start + ky * rows)]))

    owner, shifts, _ = lax.optimization_barrier((owner, shifts, by_z[near[0]]))
    (target,) = call(
        functools.partial(target_kernel, devices, ny, nz, cap),
        [VMEM],
        [struct(wide, jnp.int32)],
        [],
        10**9,
        10**6,
        "target",
    )(owner)
    target = target.reshape(BLOCKS)

    weight_keep, weight_send, squares = call(
        weigh_kernel,
        [VMEM] * 3,
        [
            struct((count, KB * BW), BF16),
            struct((count, KB * BW), BF16),
            struct((2 * ctf.shape[0], KB * BW), BF16),
        ],
        [],
        10**9,
        4 * 10**6,
        "weigh",
    )(images, groups.reshape(count, 1), ctf)
    weight_other = to(weight_send, core_pairs)
    group_row = groups.astype(F32).reshape(1, count)
    group_row = jnp.concatenate([group_row, to(group_row, core_pairs)], axis=1).astype(jnp.int32)
    place = slots.T

    lane = jnp.arange(BW)
    freq_x = (lane % HALF + core * HALF - BW // 2).astype(F32)
    freq_y = jnp.arange(KB).astype(F32)
    shift_x = shifts[:, 0].astype(F32)
    shift_y = shifts[:, 1].astype(F32)
    angles = (
        2.0
        * math.pi
        / BW
        * (
            shift_x[None, :, None] * freq_x[None, None, :]
            + shift_y[None, :, None] * freq_y[:, None, None]
        )
    )
    cosine = jnp.cos(angles)
    sine = jnp.sin(angles) * jnp.where(lane < HALF, -1.0, 1.0)

    (partial,) = call(
        functools.partial(score_kernel, [moves for _, moves in pieces]),
        [SMEM] + [VMEM] * (6 + len(pieces)),
        [struct((shift_count * R, 2 * count), F32)],
        [
            pltpu.VMEM((chips * rows + 16, BW), F32),
            pltpu.VMEM((2 * R, 2 * ctf.shape[0]), F32),
        ]
        + [pltpu.VMEM((GROUP, R, BW), F32)] * 2
        + [pltpu.VMEM((shift_count * R, GROUP * BW), BF16)] * 2
        + [pltpu.VMEM((2 * R, GROUP * BW), BF16)] * 2,
        4 * 10**9,
        10**7,
        "score",
    )(target, group_row, cosine, sine, weight_keep, weight_other, squares, *[piece for piece, _ in pieces])

    theirs = to(partial, core_pairs)
    order = near[::-1] + [0]
    outs = call(
        functools.partial(back_kernel, ny, rows, order),
        [SMEM] + [VMEM] * 6,
        [struct((1, 2 * count), F32)]
        + [struct((rows, BW), BF16)] * chips,
        [pltpu.VMEM((chips * rows + 16, BW), F32)],
        4 * 10**9,
        10**7,
        "back",
    )(target, partial, theirs, cosine, sine, weight_keep, weight_other)
    evidence = outs[0][0, :count]
    parts = {kz: outs[1 + ny * i : 1 + ny * (i + 1)] for i, kz in enumerate(order)}
    moved = {kz: [to(parts[kz][ky], along_y(ky)) for ky in range(1, ny)] for kz in order}
    crossed = {}
    for kz in order:
        total = parts[kz][0].astype(F32)
        for part in moved[kz]:
            total = total + part.astype(F32)
        crossed[kz] = to(total.astype(BF16), along_z(kz)) if kz else total

    def total_of(span):
        total = crossed[0][span]
        for kz in near[::-1]:
            total = total + crossed[kz][span].astype(F32)
        return total

    sum_other = to(total_of(slice(cap, rows)), core_pairs)
    sum_keep = total_of(slice(0, cap))

    half, spread = call(
        own_half_kernel,
        [VMEM] * 4,
        [struct((cap, 2 * BW), F32), struct((volume.shape[0], cap), BF16)],
        [],
        10**9,
        2 * 10**6,
        "own_half",
    )(place, slots, interp, sum_keep)
    (new_map,) = call(
        adjoint_kernel,
        [VMEM] * 6,
        [struct(volume.shape, F32)],
        [pltpu.VMEM(volume.shape, F32), pltpu.SemaphoreType.DMA((PARTS,))],
        10**9,
        2 * 10**6,
        "adjoint",
        40,
        ANY,
    )(slots, volume, interp, half, spread, sum_other)
    return (new_map, evidence)


def solution(mesh):
    return jax.shard_map(
        per_device,
        mesh=mesh,
        in_specs=(
            P(("parts", "img"), None),
            P(("parts", "img")),
            P("parts", None),
            P(("parts", "img"), None),
            P("parts", None),
            P("parts"),
            P("parts"),
            P(),
            P("parts", None),
        ),
        out_specs=(P(("parts", "img"), None), P(("parts", "img"))),
        check_vma=False,
    )
```

```python
import functools
import math

import jax
import jax.numpy as jnp
from jax import lax
from jax.experimental import pallas as pl
from jax.experimental.pallas import tpu as pltpu
from jax.sharding import PartitionSpec as P

BW = 128
KB = 64
R = 64
HALF = BW // 2
BLOCKS = R * KB
GROUP = 4
PARTS = 4

F32 = jnp.float32
BF16 = jnp.bfloat16
NT = (((1,), (1,)), ((), ()))
NN = (((1,), (0,)), ((), ()))


def dot(a, b, dims=NN):
    return lax.dot_general(a, b, dims, preferred_element_type=F32)


def iota(shape, axis):
    return lax.broadcasted_iota(jnp.int32, shape, axis)


def swap_halves(x):
    return pltpu.roll(x, HALF, 1)


def split_halves(real, imag):
    first = iota(real.shape, 1) < HALF
    return (
        jnp.where(first, real, swap_halves(imag)),
        jnp.where(first, swap_halves(real), imag),
    )


def triangles(rows):
    upper = jnp.where(iota((BW, BW), 0) <= iota((BW, BW), 1), 1.0, 0.0).astype(BF16)
    lower = jnp.where(iota((rows, rows), 1) < iota((rows, rows), 0), 1.0, 0.0).astype(BF16)
    return upper, jnp.ones((BW, BW), BF16), lower


def position(ny):
    me = lax.axis_index("img")
    return me, lax.shift_right_logical(me, ny.bit_length()), lax.shift_right_logical(me, 1) & (ny - 1), me & 1


def target_kernel(devices, ny, nz, cap, owner, target):
    _, z, y, core = position(ny)
    own = owner[...]
    upper, ones, lower = triangles(own.shape[0])

    def rank(d, pos):
        member = jnp.where(own == d, 1.0, 0.0)
        bits = member.astype(BF16)
        before = dot(lower, dot(bits, ones).astype(BF16))
        return pos + member * (dot(bits, upper) - 1.0 + before)

    pos = jnp.zeros(own.shape, F32)
    if devices <= 16:
        for d in range(devices):
            pos = rank(d, pos)
    else:
        pos = lax.fori_loop(0, devices, rank, pos)
    rel_core = (own & 1) ^ core
    rel_y = (lax.shift_right_logical(own, 1) - y) & (ny - 1)
    rel_z = (lax.shift_right_logical(own, ny.bit_length()) - z) & (nz - 1)
    place = ((rel_z * ny + rel_y) * 2 + rel_core) * cap + pos.astype(jnp.int32)
    ref = 2 * iota(own.shape, 0) + jnp.where(iota(own.shape, 1) < KB, 0, 1)
    place = place + 8 - (ref & 7)
    target[...] = place + pltpu.roll(place, KB, 1) * 65536


def slice_kernel(*refs):
    sources, (slots, keep, send), held, arrived = refs[:5], refs[5:8], refs[8:13], refs[13]
    copies = [
        pltpu.make_async_copy(source, place, arrived.at[i])
        for i, (source, place) in enumerate(zip(sources, held))
    ]
    for copy in copies:
        copy.start()
    owner, local, table, volume, interp = held
    me = lax.axis_index("img")
    core = me & 1
    cap = keep.shape[0]
    for copy in copies[:3]:
        copy.wait()
    own = owner[...]
    rows = own.shape[0]
    upper, ones, lower = triangles(rows)
    member = own == me
    bits = jnp.where(member, 1.0, 0.0).astype(BF16)
    total = dot(bits, ones)
    before = dot(lower, total.astype(BF16))
    pos = (dot(bits, upper) - 1.0 + before).astype(jnp.int32)
    number = iota((rows, cap), 1).astype(F32)
    start, stop = before[:, 0:1], before[:, 0:1] + total[:, 0:1]
    row_hot = jnp.where(number >= start, jnp.where(number < stop, 1.0, 0.0), 0.0)
    loc = local[...]
    fields = [
        jnp.where(member, lax.shift_right_logical(pos, 7), 255),
        pos & 127,
        lax.shift_right_logical(loc, 8),
        loc & 255,
        table[...],
    ]
    fields = jnp.concatenate([f.astype(F32) for f in fields], axis=1).astype(BF16)
    found = dot(row_hot.T.astype(BF16), fields)
    slot = iota((cap, BW), 0).astype(F32)
    valid = slot < stop[rows - 1 : rows]
    hit = found[:, :BW] * 128.0 + found[:, BW : 2 * BW] == jnp.where(valid, slot, -1.0)
    place = jnp.where(hit, found[:, 2 * BW : 3 * BW] * 256.0 + found[:, 3 * BW : 4 * BW], 0.0)
    place = jnp.sum(place, axis=1, keepdims=True)
    place = jnp.where(valid[:, 0:1], place, -1.0)
    which = jnp.sum(jnp.where(hit, found[:, 4 * BW :], 0.0), axis=1, keepdims=True)
    column = iota((cap, 8), 1)
    slots[...] = jnp.where(column == 0, place, jnp.where(column == 1, which, 0.0))

    for copy in copies[3:]:
        copy.wait()
    depth = volume.shape[0]
    pick = jnp.where(iota((cap, depth), 1) == place.astype(jnp.int32), 1.0, 0.0).astype(BF16)
    voxels = dot(pick, volume[...])
    voxels = jnp.concatenate([voxels[:, :BW], voxels[:, BW:]], axis=0)
    which = jnp.concatenate([which, which], axis=0)
    tables = range(interp.shape[0])
    chosen = [jnp.where(which == float(t), voxels, 0.0).astype(BF16) for t in tables]
    matrix = jnp.concatenate([interp[t] for t in tables], axis=1)
    out = dot(jnp.concatenate(chosen, axis=1), matrix, NT)
    left, right = split_halves(out[:cap], out[cap:])
    keep[...] = jnp.where(core == 0, left, right).astype(BF16)
    send[...] = jnp.where(core == 0, right, left).astype(BF16)


def weigh_kernel(images, group, ctf, keep, send, squares):
    core = lax.axis_index("img") & 1
    count = images.shape[0]
    groups = ctf.shape[0]
    number = jnp.broadcast_to(group[...], (count, BW))

    def body(b, carry):
        lanes = pl.ds(pl.multiple_of(b * BW, BW), BW)
        scale = ctf[:, lanes]
        factor = jnp.zeros((count, BW), F32)
        for g in range(groups):
            factor = jnp.where(number == g, scale[g : g + 1], factor)
        real = images[:, pl.ds(pl.multiple_of(b * 2 * BW, BW), BW)].astype(F32) * factor
        imag = images[:, pl.ds(pl.multiple_of(b * 2 * BW + BW, BW), BW)].astype(F32) * factor
        left, right = split_halves(real, imag)
        keep[:, lanes] = jnp.where(core == 0, left, right).astype(BF16)
        send[:, lanes] = jnp.where(core == 0, right, left).astype(BF16)
        square = scale * scale
        left, right = split_halves(square, square)
        square = jnp.where(core == 0, left, right)
        high = square.astype(BF16)
        rest = square - high.astype(F32)
        squares[:, lanes] = jnp.concatenate([high.astype(F32), rest], axis=0).astype(BF16)
        return carry

    lax.fori_loop(0, KB, body, 0, unroll=8)


def rows_of(target, r, b):
    both = target[(r // 2) * BW + b]
    return both & 65535, lax.shift_right_logical(both, 16)


def score_kernel(
    places, target, group, cosine, sine, keep, other, squares, *rest
):
    pieces = rest[: len(places)]
    scores, gathered, norms, *stages = rest[len(places) :]
    blocks, lefts, powers = stages[0:2], stages[2:4], stages[4:6]
    shifts = cosine.shape[1]
    steps = KB // GROUP
    wide = GROUP * BW
    for piece, moves in zip(pieces, places):
        for source, size, start in moves:
            gathered[start + 8 : start + 8 + size, :] = piece[source : source + size, :].astype(F32)
    scores[...] = jnp.zeros(scores.shape, F32)
    norms[...] = jnp.zeros(norms.shape, F32)

    sublane = iota((8, BW), 0)

    def fetch(b, first):
        value = None
        for r in range(first, first + 8, 2):
            for i, row in enumerate(rows_of(target, r, b)):
                loaded = gathered[pl.ds(row, 8), :]
                value = loaded if value is None else jnp.where(sublane == r + i - first, loaded, value)
        return value

    def gather(step, block):
        for part in range(GROUP):
            for first in range(0, R, 8):
                block[part, first : first + 8, :] = fetch(step * GROUP + part, first)

    def rotate(step, block, left, power):
        for part in range(GROUP):
            b = step * GROUP + part
            lanes = slice(part * BW, (part + 1) * BW)
            value = block[part]
            swapped = swap_halves(value)
            for s in range(shifts):
                turned = value * cosine[b, s : s + 1, :] + swapped * sine[b, s : s + 1, :]
                left[s * R : (s + 1) * R, lanes] = turned.astype(BF16)
            square = value * value
            high = square.astype(BF16)
            power[0:R, lanes] = high
            power[R : 2 * R, lanes] = (square - high.astype(F32)).astype(BF16)

    def multiply(step, left, power):
        lanes = pl.ds(pl.multiple_of(step * wide, wide), wide)
        right = jnp.concatenate([keep[:, lanes], other[:, lanes]], axis=0)
        scores[...] += dot(left[...], right, NT)
        norms[...] += dot(power[...], squares[:, lanes], NT)

    def body(pair, carry):
        for half in range(2):
            step = 2 * pair + half
            gather(jnp.minimum(step + 1, steps - 1), blocks[1 - half])
            rotate(step, blocks[half], lefts[half], powers[half])
            multiply(jnp.maximum(step - 1, 0), lefts[1 - half], powers[1 - half])
        return carry

    gather(0, blocks[0])
    lefts[1][...] = jnp.zeros(lefts[1].shape, BF16)
    powers[1][...] = jnp.zeros(powers[1].shape, BF16)
    lax.fori_loop(0, steps // 2, body, 0)
    multiply(steps - 1, lefts[1], powers[1])
    half = squares.shape[0] // 2
    total = norms[...]
    total = total[:R, :half] + total[:R, half:] + total[R:, :half] + total[R:, half:]
    norm = jnp.zeros((R, scores.shape[1]), F32)
    for g in range(half):
        norm = jnp.where(group[...] == g, total[:, g : g + 1], norm)
    for s in range(shifts):
        scores[s * R : (s + 1) * R, :] -= 0.5 * norm


def back_kernel(ny, rows, order, target, mine, theirs, cosine, sine, keep, other, *rest):
    evidence = rest[0]
    placed = rest[-1]
    shifts = cosine.shape[1]
    scale = 1.0 / math.sqrt(KB * BW)
    placed[...] = jnp.zeros(placed.shape, F32)
    scores = (mine[...] + swap_halves(theirs[...])) * scale
    top = jnp.max(scores, axis=0, keepdims=True)
    exponent = jnp.exp(scores - top)
    total = jnp.sum(exponent, axis=0, keepdims=True)
    evidence[...] = (top + jnp.log(total))[:, : evidence.shape[1]]
    weights = (exponent / total).astype(BF16)
    sublane = iota((8, BW), 0)

    def body(pair, carry):
        lanes = pl.ds(pl.multiple_of(pair * 2 * BW, BW), 2 * BW)
        right = jnp.concatenate([keep[:, lanes], other[:, lanes]], axis=0)
        sums = dot(weights, right)
        for part in range(2):
            b = pair * 2 + part
            straight = jnp.zeros((R, BW), F32)
            crossed = jnp.zeros((R, BW), F32)
            for s in range(shifts):
                term = sums[s * R : (s + 1) * R, part * BW : (part + 1) * BW]
                straight = straight + term * cosine[b, s : s + 1, :]
                crossed = crossed + term * sine[b, s : s + 1, :]
            value = straight + swap_halves(crossed)
            for r in range(0, R, 2):
                for i, row in enumerate(rows_of(target, r, b)):
                    k = (r + i) % 8
                    pltpu.store(
                        placed.at[pl.ds(row, 8), :],
                        value[r + i - k : r + i - k + 8],
                        mask=sublane == k,
                    )
        return carry

    lax.fori_loop(0, KB // 2, body, 0, unroll=4)
    for i, kz in enumerate(order):
        for ky in range(ny):
            start = (kz * ny + ky) * rows + 8
            rest[1 + i * ny + ky][...] = placed[start : start + rows, :].astype(BF16)


def interpolate_back(value, slots, interp, core):
    which = jnp.broadcast_to(slots[:, 1:2], value.shape)
    tables = range(interp.shape[0])
    blank = jnp.zeros((HALF, BW), BF16)
    matrix = []
    for t in tables:
        half = jnp.where(core == 0, interp[t][:HALF], interp[t][HALF:])
        matrix += [jnp.concatenate(pair, axis=1) for pair in ((half, blank), (blank, half))]
    matrix = jnp.concatenate(matrix, axis=0)
    high = value.astype(BF16).astype(F32)
    out = jnp.zeros((value.shape[0], 2 * BW), F32)
    for part in (high, value - high):
        chosen = [jnp.where(which == float(t), part, 0.0).astype(BF16) for t in tables]
        out = out + dot(jnp.concatenate(chosen, axis=1), matrix)
    return out


def own_half_kernel(place, slots, interp, keep, half, spread):
    core = lax.axis_index("img") & 1
    half[...] = interpolate_back(keep[...], slots, interp, core)
    spread[...] = jnp.where(
        iota(spread.shape, 0) == place[0:1, :].astype(jnp.int32), 1.0, 0.0
    ).astype(BF16)


def adjoint_kernel(slots, volume, interp, half, spread, other, new_map, held, sent):
    core = lax.axis_index("img") & 1
    out = half[...] + interpolate_back(other[...], slots, interp, 1 - core)
    high = out.astype(BF16)
    rest = (out - high.astype(F32)).astype(BF16)
    sums = jnp.concatenate([high, rest], axis=0)
    size = volume.shape[0] // PARTS
    copies = []
    for part in range(PARTS):
        rows = slice(part * size, (part + 1) * size)
        hot = spread[rows, :]
        held[rows, :] = volume[rows, :].astype(F32) + dot(
            jnp.concatenate([hot, hot], axis=1), sums
        )
        copy = pltpu.make_async_copy(held.at[rows, :], new_map.at[rows, :], sent.at[part])
        copy.start()
        copies.append(copy)
    for copy in copies:
        copy.wait()


SMEM = pl.BlockSpec(memory_space=pltpu.SMEM)
VMEM = pl.BlockSpec(memory_space=pltpu.VMEM)
ANY = pl.BlockSpec(memory_space=pl.ANY)


def call(kernel, in_specs, out_shapes, scratch, flops, touched, name, limit=40, out=VMEM):
    return pl.pallas_call(
        kernel,
        in_specs=in_specs,
        out_specs=[out] * len(out_shapes),
        out_shape=out_shapes,
        scratch_shapes=scratch,
        compiler_params=pltpu.CompilerParams(vmem_limit_bytes=limit * 1024 * 1024),
        cost_estimate=pl.CostEstimate(flops=flops, bytes_accessed=touched, transcendentals=0),
        name=name,
    )


def per_device(images, groups, shifts, volume, owner, local, table_id, interp, ctf):
    devices = lax.axis_size("img")
    chips = devices // 2
    ny = 1 << ((chips.bit_length() - 1) // 2)
    nz = chips // ny
    me = lax.axis_index("img")
    core = me % 2
    cap = max(2, 3 * BLOCKS // (2 * devices))
    rows = 2 * cap
    count = images.shape[0]
    shift_count = shifts.shape[0]
    struct = jax.ShapeDtypeStruct

    def device(dz, dy, dc):
        return (dz * ny + dy) * 2 + dc

    everyone = [(dz, dy, dc) for dz in range(nz) for dy in range(ny) for dc in range(2)]
    core_pairs = [(device(*d), device(d[0], d[1], 1 - d[2])) for d in everyone]

    def along_z(k):
        return [(device(a, b, c), device((a + k) % nz, b, c)) for a, b, c in everyone]

    def along_y(k):
        return [(device(a, b, c), device(a, (b + k) % ny, c)) for a, b, c in everyone]

    def to(array, pairs):
        return lax.ppermute(array, "img", pairs)

    wide = (BLOCKS // BW, BW)
    owner = owner.reshape(wide)
    slots, slice_keep, slice_send = call(
        slice_kernel,
        [ANY] * 5,
        [struct((cap, 8), F32), struct((cap, BW), BF16), struct((cap, BW), BF16)],
        [pltpu.VMEM(wide, jnp.int32)] * 3
        + [
            pltpu.VMEM(volume.shape, BF16),
            pltpu.VMEM(interp.shape, BF16),
            pltpu.SemaphoreType.DMA((5,)),
        ],
        10**9,
        10**6,
        "own_slices",
        60,
    )(owner, local.reshape(wide), table_id.reshape(wide), volume, interp)
    own_piece = jnp.concatenate([slice_keep, to(slice_send, core_pairs)], axis=0)
    images, groups, _ = lax.optimization_barrier((images, groups, own_piece))

    near = sorted(range(1, nz), key=lambda k: min(k, nz - k))
    pieces = [(own_piece, [(0, rows, 0)])]
    by_z = {kz: to(own_piece, along_z(-kz)) for kz in near}
    for ky in range(1, ny):
        pieces.append((to(own_piece, along_y(-ky)), [(0, rows, ky * rows)]))
    for kz in near:
        start = kz * ny * rows
        pieces.append((by_z[kz], [(0, rows, start)]))
        for ky in range(1, ny):
            piece = to(by_z[kz], along_y(-ky))
            pieces.append((piece, [(0, rows, start + ky * rows)]))

    owner, shifts, _ = lax.optimization_barrier((owner, shifts, by_z[near[0]]))
    (target,) = call(
        functools.partial(target_kernel, devices, ny, nz, cap),
        [VMEM],
        [struct(wide, jnp.int32)],
        [],
        10**9,
        10**6,
        "target",
    )(owner)
    target = target.reshape(BLOCKS)

    weight_keep, weight_send, squares = call(
        weigh_kernel,
        [VMEM] * 3,
        [
            struct((count, KB * BW), BF16),
            struct((count, KB * BW), BF16),
            struct((2 * ctf.shape[0], KB * BW), BF16),
        ],
        [],
        10**9,
        4 * 10**6,
        "weigh",
    )(images, groups.reshape(count, 1), ctf)
    weight_other = to(weight_send, core_pairs)
    group_row = groups.astype(F32).reshape(1, count)
    group_row = jnp.concatenate([group_row, to(group_row, core_pairs)], axis=1).astype(jnp.int32)
    place = slots.T

    lane = jnp.arange(BW)
    freq_x = (lane % HALF + core * HALF - BW // 2).astype(F32)
    freq_y = jnp.arange(KB).astype(F32)
    shift_x = shifts[:, 0].astype(F32)
    shift_y = shifts[:, 1].astype(F32)
    angles = (
        2.0
        * math.pi
        / BW
        * (
            shift_x[None, :, None] * freq_x[None, None, :]
            + shift_y[None, :, None] * freq_y[:, None, None]
        )
    )
    cosine = jnp.cos(angles)
    sine = jnp.sin(angles) * jnp.where(lane < HALF, -1.0, 1.0)

    (partial,) = call(
        functools.partial(score_kernel, [moves for _, moves in pieces]),
        [SMEM] + [VMEM] * (6 + len(pieces)),
        [struct((shift_count * R, 2 * count), F32)],
        [
            pltpu.VMEM((chips * rows + 16, BW), F32),
            pltpu.VMEM((2 * R, 2 * ctf.shape[0]), F32),
        ]
        + [pltpu.VMEM((GROUP, R, BW), F32)] * 2
        + [pltpu.VMEM((shift_count * R, GROUP * BW), BF16)] * 2
        + [pltpu.VMEM((2 * R, GROUP * BW), BF16)] * 2,
        4 * 10**9,
        10**7,
        "score",
    )(target, group_row, cosine, sine, weight_keep, weight_other, squares, *[piece for piece, _ in pieces])

    theirs = to(partial, core_pairs)
    order = near[::-1] + [0]
    outs = call(
        functools.partial(back_kernel, ny, rows, order),
        [SMEM] + [VMEM] * 6,
        [struct((1, count), F32)]
        + [struct((rows, BW), BF16)] * chips,
        [pltpu.VMEM((chips * rows + 16, BW), F32)],
        4 * 10**9,
        10**7,
        "back",
    )(target, partial, theirs, cosine, sine, weight_keep, weight_other)
    evidence = outs[0].reshape(count)
    parts = {kz: outs[1 + ny * i : 1 + ny * (i + 1)] for i, kz in enumerate(order)}
    moved = {kz: [to(parts[kz][ky], along_y(ky)) for ky in range(1, ny)] for kz in order}
    crossed = {}
    for kz in order:
        total = parts[kz][0].astype(F32)
        for part in moved[kz]:
            total = total + part.astype(F32)
        crossed[kz] = to(total.astype(BF16), along_z(kz)) if kz else total

    def total_of(span):
        total = crossed[0][span]
        for kz in near[::-1]:
            total = total + crossed[kz][span].astype(F32)
        return total

    sum_other = to(total_of(slice(cap, rows)), core_pairs)
    sum_keep = total_of(slice(0, cap))

    half, spread = call(
        own_half_kernel,
        [VMEM] * 4,
        [struct((cap, 2 * BW), F32), struct((volume.shape[0], cap), BF16)],
        [],
        10**9,
        2 * 10**6,
        "own_half",
    )(place, slots, interp, sum_keep)
    (new_map,) = call(
        adjoint_kernel,
        [VMEM] * 6,
        [struct(volume.shape, F32)],
        [pltpu.VMEM(volume.shape, F32), pltpu.SemaphoreType.DMA((PARTS,))],
        10**9,
        2 * 10**6,
        "adjoint",
        40,
        ANY,
    )(slots, volume, interp, half, spread, sum_other)
    return (new_map, evidence)


def solution(mesh):
    return jax.shard_map(
        per_device,
        mesh=mesh,
        in_specs=(
            P(("parts", "img"), None),
            P(("parts", "img")),
            P("parts", None),
            P(("parts", "img"), None),
            P("parts", None),
            P("parts"),
            P("parts"),
            P(),
            P("parts", None),
        ),
        out_specs=(P(("parts", "img"), None), P(("parts", "img"))),
        check_vma=False,
    )
```
